128 devices in a mesh: row: 4 (over x), col: 32 (over y, z, core).
Axes of the slice: x: 4, y: 4, z: 4, core: 2. Of those that a mesh axis runs over, the one named last changes fastest.
Arguments:
- pair_slab: bfloat16 [32, 4096, 128], P('row', 'col'), may hold values from -6 to 6
- pair_bias: bfloat16 [4, 4096, 4096], P(None, 'col', 'row'), may hold values from -5 to 240
- tile_mask: int32 [64, 64], replicated, may hold values from 0 to 1, as said below
- w_proj: bfloat16 [128, 512], replicated, may hold values from -0.5 to 0.5
- w_out: bfloat16 [128, 128], replicated, may hold values from -0.5 to 0.5
- d_out: bfloat16 [32, 4096, 128], P('row', 'col'), may hold values from -6 to 6
Outputs:
- attn_out: bfloat16 [32, 4096, 128], P('row', 'col')
- slab_grads: bfloat16 [32, 4096, 128], P('row', 'col')
- bias_grads: float32 [4096, 4, 4096], P(('row', 'col'))
The draws below stay inside these ranges and needn't reach their ends.
Inputs may be any that keep to these rules, and one draw needn't show every extreme that they name: tile_mask[a, a] is 1 for every tile a, and tile_mask[a, b] is 0 wherever b > a.
All inputs are finite; a program needn't handle non-finite values.
Results may differ from the reference program's by a relative error of at most 0.019.
Values may be sent and summed in bfloat16 or wider, within the bound.
A program may use at most 192 MiB of HBM per device.

```python
import jax
import jax.numpy as jnp
from jax import lax

C = 128
H = 4
DH = 32
TILE = 64
N = 4096
SLAB = 32


def draw_pair_bias(key, part):
    values = jnp.clip(jax.random.normal(key, (H, N, N), jnp.float32), -5.0, 5.0)
    return values.astype(jnp.bfloat16)


def draw_tile_mask(key, part):
    tile_count = N // TILE
    coins = jax.random.randint(key, (tile_count, tile_count), 0, 2, jnp.int32)
    query_ids = lax.broadcasted_iota(jnp.int32, (tile_count, tile_count), 0)
    key_ids = lax.broadcasted_iota(jnp.int32, (tile_count, tile_count), 1)
    return jnp.where(key_ids == query_ids, 1, jnp.where(key_ids < query_ids, coins, 0)).astype(jnp.int32)


def block_scale(own_key, dims, shards, low, largest):
    level = 1.0
    for dim, blocks in shards:
        steps = jax.random.uniform(jax.random.fold_in(jax.random.fold_in(own_key, 6), dim), (blocks,), jnp.float32, low / len(shards), largest / len(shards))
        level = level * jnp.repeat(jnp.exp(steps), dims[dim] // blocks).reshape((-1,) + (1,) * (len(dims) - 1 - dim))
    return level


def scatter_about(rng, dims, width, most, pieces=(), dtype=jnp.bfloat16):
    gain = block_scale(rng, dims, pieces, -0.22, 0.18) if pieces else 1.0
    result = jax.random.normal(rng, dims, jnp.float32) * width * gain
    return jnp.minimum(jnp.maximum(result, -most), most).astype(dtype)


def setup_inputs(seed: int = 0) -> dict:
    streams_of = jax.random.split(jax.random.key(seed), 7)
    pair_slab = scatter_about(streams_of[0], (SLAB, N, C), 1.0, 6.0, ((0, 4), (1, 32)))
    pair_bias = draw_pair_bias(jax.random.fold_in(streams_of[6], 71), 0)
    tile_mask = draw_tile_mask(jax.random.fold_in(streams_of[6], 71), 0)
    w_proj = scatter_about(streams_of[3], (C, 4 * H * DH), C ** -0.5, 0.5)
    w_out = scatter_about(streams_of[4], (H * DH, C), (H * DH) ** -0.5, 0.5)
    d_out = scatter_about(streams_of[5], (SLAB, N, C), 1.0, 6.0, ((0, 4), (1, 32)))
    return dict(pair_slab=pair_slab, pair_bias=pair_bias, tile_mask=tile_mask, w_proj=w_proj, w_out=w_out, d_out=d_out)


eps_norm = 1e-05
neg_big = -1e+30

def normalize(pair_slab):
    entries = pair_slab.astype(jnp.float32)
    centred = entries - lax.optimization_barrier(jnp.mean(entries, axis=-1, keepdims=True))
    spread = lax.optimization_barrier(jnp.mean(centred * centred, axis=-1, keepdims=True))
    return centred * lax.rsqrt(spread + eps_norm)

def round_trip(value):
    return lax.optimization_barrier(value.astype(jnp.bfloat16)).astype(jnp.float32)

def reference(pair_slab, pair_bias, tile_mask, w_proj, w_out, d_out):
    slab_rows, total_cols, channels = pair_slab.shape
    head_width = H * DH
    q_scale = DH ** (-0.5)
    normed_f, norm_pull = jax.vjp(normalize, pair_slab)
    normed = normed_f.astype(jnp.bfloat16)
    projected = jnp.dot(normed.reshape(-1, channels), w_proj, preferred_element_type=jnp.float32)
    projected = projected.reshape(slab_rows, total_cols, 4 * head_width)
    queries = (projected[..., :head_width] * q_scale).astype(jnp.bfloat16)
    key_proj = projected[..., head_width:2 * head_width].astype(jnp.bfloat16)
    value_proj = projected[..., 2 * head_width:3 * head_width].astype(jnp.bfloat16)
    gating = jax.nn.sigmoid(projected[..., 3 * head_width:])
    active = (jnp.repeat(jnp.repeat(tile_mask, TILE, axis=0), TILE, axis=1) > 0)[None]
    bias_full = pair_bias.astype(jnp.float32)

    def heads_of(row_values):
        return row_values.astype(jnp.float32).reshape(total_cols, H, DH)

    def row_logits(query_row, key_row):
        return jnp.einsum('jhd,khd->hjk', heads_of(query_row), heads_of(key_row)) + bias_full

    def forward_row(inputs):
        query_row, key_row, value_row = inputs
        logits = jnp.where(active, row_logits(query_row, key_row), neg_big)
        row_max = lax.optimization_barrier(jnp.max(logits, axis=-1, keepdims=True))
        exp_total = lax.optimization_barrier(jnp.sum(jnp.where(active, jnp.exp(logits - row_max), 0.0), axis=-1, keepdims=True))
        log_norm = row_max + jnp.log(exp_total)
        weights = round_trip(jnp.where(active, jnp.exp(logits - log_norm), 0.0))
        attended = jnp.einsum('hjk,khd->jhd', weights, heads_of(value_row))
        return (attended.reshape(total_cols, head_width), log_norm[..., 0])
    attended, log_norm = lax.map(forward_row, (queries, key_proj, value_proj))
    gated = (gating * attended).astype(jnp.bfloat16)
    attn_out = jnp.dot(gated.reshape(-1, head_width), w_out, preferred_element_type=jnp.float32)
    attn_out = attn_out.astype(jnp.bfloat16).reshape(slab_rows, total_cols, channels)
    d_gated = jnp.dot(d_out.reshape(-1, channels), jnp.transpose(w_out), preferred_element_type=jnp.float32)
    d_gated = d_gated.reshape(slab_rows, total_cols, head_width)
    d_attended = (d_gated * gating).astype(jnp.bfloat16)
    d_gate_lin = d_gated * attended * gating * (1.0 - gating)
    row_delta = lax.optimization_barrier(jnp.sum((d_attended.astype(jnp.float32) * attended).reshape(slab_rows, total_cols, H, DH), axis=-1))
    row_delta = jnp.transpose(row_delta, (0, 2, 1))

    def backward_row(bias_acc, inputs):
        query_row, key_row, value_row, datt_row, norm_row, delta_row = inputs
        logits = row_logits(query_row, key_row)
        probs = jnp.where(active, jnp.exp(logits - norm_row[..., None]), 0.0)
        weights = round_trip(probs)
        d_probs = jnp.einsum('jhd,khd->hjk', heads_of(datt_row), heads_of(value_row))
        d_logits = probs * (d_probs - delta_row[..., None])
        d_logits_b = round_trip(d_logits)
        d_query = jnp.einsum('hjk,khd->jhd', d_logits_b, heads_of(key_row)).reshape(total_cols, head_width)
        d_keys = jnp.einsum('hjk,jhd->khd', d_logits_b, heads_of(query_row)).reshape(total_cols, head_width)
        d_values = jnp.einsum('hjk,jhd->khd', weights, heads_of(datt_row)).reshape(total_cols, head_width)
        return (bias_acc + d_logits, (d_query, d_keys, d_values))
    bias_start = jnp.zeros((H, total_cols, total_cols), jnp.float32)
    bias_acc, row_grads = lax.scan(backward_row, bias_start, (queries, key_proj, value_proj, d_attended, log_norm, row_delta))
    d_query, d_keys, d_values = row_grads
    d_qg = jnp.concatenate([d_query * q_scale, d_gate_lin], axis=-1).astype(jnp.bfloat16).reshape(-1, 2 * head_width)
    w_qg = jnp.concatenate([w_proj[:, :head_width], w_proj[:, 3 * head_width:]], axis=1)
    w_pair_back = jnp.transpose(w_proj[:, head_width:3 * head_width]).astype(jnp.float32)
    pair_grads = jnp.concatenate([d_keys, d_values], axis=-1).reshape(-1, 2 * head_width)
    d_normed = jnp.dot(d_qg, jnp.transpose(w_qg), preferred_element_type=jnp.float32)
    d_normed = d_normed + jnp.dot(pair_grads, w_pair_back, precision=lax.Precision.HIGHEST)
    slab_grads = norm_pull(d_normed.reshape(slab_rows, total_cols, channels))[0]
    bias_grads = jnp.transpose(bias_acc, (2, 0, 1))
    return (attn_out, slab_grads, bias_grads)
```

```python
import functools

import jax
import jax.numpy as jnp
from jax import lax
from jax.experimental import pallas as pl
from jax.experimental.pallas import tpu as pltpu
from jax.sharding import PartitionSpec as P

H = 4
DH = 32
TILE = 64
HJ = H * TILE

eps_norm = 1e-05
neg_big = -1e30
CT = 4
F32 = jnp.float32
BF16 = jnp.bfloat16


def nt(a, b):
    return lax.dot_general(a, b, (((1,), (1,)), ((), ())), preferred_element_type=F32)


def tn(a, b):
    return lax.dot_general(a, b, (((0,), (0,)), ((), ())), preferred_element_type=F32)


def nn(a, b):
    return jnp.dot(a, b, preferred_element_type=F32)


def head_blocks(rows, chans):
    row_head = lax.broadcasted_iota(jnp.int32, (rows, chans), 0) // TILE
    col_head = lax.broadcasted_iota(jnp.int32, (rows, chans), 1) // DH
    return row_head == col_head


def diagonal(full_t):
    parts = [full_t[h * DH : (h + 1) * DH, h * TILE : (h + 1) * TILE] for h in range(H)]
    return jnp.transpose(jnp.concatenate(parts, axis=0))


def attention_kernel(
    place_ref, mask_ref, x_ref, bias_ref, d_out_ref, w_proj_ref, w_out_ref,
    out_ref, dn_ref, pair_ref, bias_grad_ref,
    k_ref, v_ref, q_ref, do_ref, bias_f, grad_f, max_ref, sum_ref, delta_ref, acc_ref,
    gate_ref, dg_ref, list_ref,
):
    c = place_ref[0]
    tiles = 2 * x_ref.shape[0]
    rows = x_ref.shape[1]
    width = H * DH
    q_scale = DH ** (-0.5)
    query_tiles = (2 * c, tiles - 1 - 2 * c)
    w_q = w_proj_ref[:, :width]
    w_pair = w_proj_ref[:, width : 3 * width]
    w_gate = w_proj_ref[:, 3 * width :]

    def project(block, _):
        for r in range(rows):
            kv = nn(x_ref[block, r], w_pair).astype(BF16)
            for half in range(2):
                k_ref[2 * block + half, r] = kv[half * TILE : (half + 1) * TILE, :width]
                v_ref[2 * block + half, r] = kv[half * TILE : (half + 1) * TILE, width:]
        return 0

    lax.fori_loop(0, jnp.maximum(c, tiles // 2 - 1 - c) + 1, project, 0)

    counts, idles = [], []
    for a in range(2):
        def scan_tile(b, carried, a=a):
            count, idle = carried
            live = mask_ref[query_tiles[a], b] > 0
            list_ref[a, count] = b
            return jnp.where(live, count + 1, count), jnp.where(live, idle, b)

        count, idle = lax.fori_loop(0, tiles, scan_tile, (jnp.int32(0), jnp.int32(0)))
        for extra in range(CT):
            list_ref[a, count + extra] = query_tiles[a]
        counts.append(count)
        idles.append(idle)

    blocks = head_blocks(HJ, width)
    for a in range(2):
        tile = query_tiles[a]

        def prepare(r, _, a=a, tile=tile):
            x_q = x_ref[tile // 2, r, pl.ds(pl.multiple_of((tile % 2) * TILE, TILE), TILE), :]
            queries = (nn(x_q, w_q) * q_scale).astype(BF16)
            gating = jax.nn.sigmoid(nn(x_q, w_gate))
            d_gated = nt(d_out_ref[a, r], w_out_ref[...])
            d_att = (d_gated * gating).astype(BF16)
            zero = jnp.zeros((HJ, width), BF16)
            q_ref[a, r] = jnp.where(blocks, jnp.concatenate([queries] * H, axis=0), zero)
            do_ref[a, r] = jnp.where(blocks, jnp.concatenate([d_att] * H, axis=0), zero)
            gate_ref[a, r] = gating
            dg_ref[a, r] = d_gated
            return 0

        lax.fori_loop(0, rows, prepare, 0)

    def load_chunk(a, n):
        ids = [list_ref[a, n * CT + t] for t in range(CT)]
        for t in range(CT):
            block = bias_ref[a, ids[t]].astype(F32)
            shut = jnp.where(n * CT + t < counts[a], 0.0, neg_big)
            bias_f[t * TILE : (t + 1) * TILE, :] = block + shut
        return ids

    max_ref[...] = jnp.full(max_ref.shape, neg_big, F32)
    sum_ref[...] = jnp.zeros(sum_ref.shape, F32)
    acc_ref[...] = jnp.zeros(acc_ref.shape, F32)
    for a in range(2):
        def forward(n, _, a=a):
            ids = load_chunk(a, n)

            def per_row(r):
                keys = jnp.concatenate([k_ref[i, r] for i in ids], axis=0)
                values = jnp.concatenate([v_ref[i, r] for i in ids], axis=0)
                scores = nt(keys, q_ref[a, r]) + bias_f[...]
                old = max_ref[a, r]
                new = jnp.maximum(old, jnp.max(scores, axis=0, keepdims=True))
                fade = jnp.exp(old - new)
                probs = jnp.exp(scores - new)
                max_ref[a, r] = new
                sum_ref[a, r] = sum_ref[a, r] * fade + jnp.sum(probs, axis=0, keepdims=True)
                acc_ref[a, r] = acc_ref[a, r] * fade + tn(values, probs.astype(BF16))

            def some_rows(step, _):
                for u in range(2):
                    per_row(step * 2 + u)
                return 0

            lax.fori_loop(0, rows // 2, some_rows, 0)
            return 0

        lax.fori_loop(0, (counts[a] + CT - 1) // CT, forward, 0)

    for a in range(2):
        def middle(r, _, a=a):
            total = sum_ref[a, r]
            full_t = acc_ref[a, r] * (1.0 / total)
            max_ref[a, r] = max_ref[a, r] + jnp.log(total)
            delta_ref[a, r] = jnp.sum(
                full_t * jnp.transpose(do_ref[a, r].astype(F32)), axis=0, keepdims=True
            )
            attended = diagonal(full_t)
            gating = gate_ref[a, r]
            gated = (gating * attended).astype(BF16)
            out_ref[a, r] = nn(gated, w_out_ref[...]).astype(BF16)
            dg_ref[a, r] = dg_ref[a, r] * attended * gating * (1.0 - gating)
            acc_ref[a, r] = jnp.zeros(acc_ref.shape[2:], F32)
            return 0

        lax.fori_loop(0, rows, middle, 0)

    def clear(b, _):
        pair_ref[b] = jnp.zeros(pair_ref.shape[1:], BF16)
        for a in range(2):
            bias_grad_ref[a, b] = jnp.zeros(bias_grad_ref.shape[2:], BF16)
        return 0

    lax.fori_loop(0, tiles, clear, 0)
    for a in range(2):
        def backward(n, _, a=a):
            ids = load_chunk(a, n)

            def per_row(r, first):
                keys = jnp.concatenate([k_ref[i, r] for i in ids], axis=0)
                values = jnp.concatenate([v_ref[i, r] for i in ids], axis=0)
                q = q_ref[a, r]
                do = do_ref[a, r]
                probs = jnp.exp(nt(keys, q) + bias_f[...] - max_ref[a, r])
                d_scores = probs * (nt(values, do) - delta_ref[a, r])
                if first is None:
                    grad_f[...] += d_scores
                else:
                    grad_f[...] = jnp.where(first, d_scores, grad_f[...] + d_scores)
                d_b = d_scores.astype(BF16)
                acc_ref[a, r] += tn(keys, d_b)
                d_keys = nn(d_b, q)
                d_values = nn(probs.astype(BF16), do)
                both = jnp.concatenate([d_keys, d_values], axis=1).astype(BF16)
                term = nt(both, w_pair)
                for t in range(CT):
                    piece = term[t * TILE : (t + 1) * TILE]
                    pair_ref[ids[t], r] = (pair_ref[ids[t], r].astype(F32) + piece).astype(BF16)

            def some_rows(step, _):
                for u in range(2):
                    per_row(step * 2 + u, (step == 0) if u == 0 else None)
                return 0

            lax.fori_loop(0, rows // 2, some_rows, 0)
            for t in range(CT):
                target = jnp.where(n * CT + t < counts[a], ids[t], idles[a])
                bias_grad_ref[a, target] = grad_f[t * TILE : (t + 1) * TILE, :].astype(BF16)
            return 0

        lax.fori_loop(0, (counts[a] + CT - 1) // CT, backward, 0)

    for a in range(2):
        def finish(r, _, a=a):
            d_q = diagonal(acc_ref[a, r]) * q_scale
            d_q = nt(d_q.astype(BF16), w_q)
            dn_ref[a, r] = (d_q + nt(dg_ref[a, r].astype(BF16), w_gate)).astype(BF16)
            return 0

        lax.fori_loop(0, rows, finish, 0)


def attention(place, mask, x_all, bias_t, d_out, w_proj, w_out):
    blocks, rows, cols, chans = x_all.shape
    tiles = blocks * cols // TILE
    width = H * DH
    vmem = pl.BlockSpec(memory_space=pltpu.VMEM)
    smem = pl.BlockSpec(memory_space=pltpu.SMEM)
    return pl.pallas_call(
        attention_kernel,
        out_shape=(
            jax.ShapeDtypeStruct((2, rows, TILE, chans), BF16),
            jax.ShapeDtypeStruct((2, rows, TILE, chans), BF16),
            jax.ShapeDtypeStruct((tiles, rows, TILE, chans), BF16),
            jax.ShapeDtypeStruct((2, tiles, TILE, HJ), BF16),
        ),
        in_specs=[smem, smem, vmem, vmem, vmem, vmem, vmem],
        out_specs=(vmem,) * 4,
        scratch_shapes=[
            pltpu.VMEM((tiles, rows, TILE, width), BF16),
            pltpu.VMEM((tiles, rows, TILE, width), BF16),
            pltpu.VMEM((2, rows, HJ, width), BF16),
            pltpu.VMEM((2, rows, HJ, width), BF16),
            pltpu.VMEM((CT * TILE, HJ), F32),
            pltpu.VMEM((CT * TILE, HJ), F32),
            pltpu.VMEM((2, rows, 1, HJ), F32),
            pltpu.VMEM((2, rows, 1, HJ), F32),
            pltpu.VMEM((2, rows, 1, HJ), F32),
            pltpu.VMEM((2, rows, width, HJ), F32),
            pltpu.VMEM((2, rows, TILE, width), F32),
            pltpu.VMEM((2, rows, TILE, width), F32),
            pltpu.SMEM((2, tiles + CT), jnp.int32),
        ],
        compiler_params=pltpu.CompilerParams(vmem_limit_bytes=60 * 1024 * 1024),
        name="attention",
    )(place, mask, x_all, bias_t, d_out, w_proj, w_out)


def on_device(pair_slab, pair_bias, tile_mask, w_proj, w_out, d_out):
    rows, cols, chans = pair_slab.shape
    ncol = lax.axis_size("col")
    flip = [(i, ncol - 1 - i) for i in range(ncol)]
    c = lax.axis_index("col")
    entries = pair_slab.astype(F32)
    centred = entries - jnp.mean(entries, axis=-1, keepdims=True)
    spread = jnp.mean(centred * centred, axis=-1, keepdims=True)
    rstd = lax.rsqrt(spread + eps_norm)
    normed_f = centred * rstd
    x_all = lax.all_gather(normed_f.astype(BF16), "col", axis=0)

    halves = pair_bias.reshape(H, 2, TILE, -1).transpose(1, 3, 0, 2).reshape(2, -1, HJ)
    bias_pair = jnp.stack([halves[0], lax.ppermute(halves[1], "col", flip)])
    bias_t = lax.all_gather(bias_pair, "row", axis=1, tiled=True)
    bias_t = bias_t.reshape(2, -1, TILE, HJ)
    d_out_h = d_out.reshape(rows, 2, TILE, chans).transpose(1, 0, 2, 3)
    d_out_pair = jnp.stack([d_out_h[0], lax.ppermute(d_out_h[1], "col", flip)])

    out, dn, pair, bias_grad = attention(
        c.reshape(1).astype(jnp.int32), tile_mask, x_all, bias_t, d_out_pair, w_proj, w_out
    )

    out_odd = lax.ppermute(out[1], "col", flip)
    attn_out = jnp.stack([out[0], out_odd], axis=1).reshape(rows, cols, chans)
    dn_odd = lax.ppermute(dn[1], "col", flip)
    dn_own = jnp.stack([dn[0], dn_odd], axis=1).reshape(rows, cols, chans).astype(F32)
    pair_sum = lax.psum_scatter(pair, "col", scatter_dimension=0, tiled=True)
    pair_sum = pair_sum.transpose(1, 0, 2, 3).reshape(rows, cols, chans)
    d_normed = dn_own + pair_sum.astype(F32)
    slab_grads = rstd * (
        d_normed
        - jnp.mean(d_normed, axis=-1, keepdims=True)
        - normed_f * jnp.mean(d_normed * normed_f, axis=-1, keepdims=True)
    )
    grads = bias_grad.reshape(2, -1, HJ)
    grads = lax.psum_scatter(grads, "row", scatter_dimension=1, tiled=True)
    grads = grads.reshape(2, ncol, -1, H, TILE)
    grads = lax.all_to_all(grads, "col", split_axis=1, concat_axis=1, tiled=True)
    even = grads[0]
    odd = grads[1][::-1]
    both = jnp.stack([even, odd], axis=1).astype(F32)
    bias_grads = both.transpose(2, 3, 0, 1, 4).reshape(-1, H, ncol * cols)
    return attn_out, slab_grads.astype(BF16), bias_grads


def solution(mesh):
    in_specs = (P("row", "col", None), P(None, "col", "row"), P(), P(), P(), P("row", "col", None))
    out_specs = (P("row", "col", None), P("row", "col", None), P(("row", "col"), None, None))
    return jax.shard_map(
        on_device, mesh=mesh, in_specs=in_specs, out_specs=out_specs, check_vma=False
    )
```

```python
import functools

import jax
import jax.numpy as jnp
from jax import lax
from jax.experimental import pallas as pl
from jax.experimental.pallas import tpu as pltpu
from jax.sharding import PartitionSpec as P

H = 4
DH = 32
TILE = 64
HJ = H * TILE

eps_norm = 1e-05
neg_big = -1e30
CT = 4
F32 = jnp.float32
BF16 = jnp.bfloat16


def nt(a, b):
    return lax.dot_general(a, b, (((1,), (1,)), ((), ())), preferred_element_type=F32)


def tn(a, b):
    return lax.dot_general(a, b, (((0,), (0,)), ((), ())), preferred_element_type=F32)


def nn(a, b):
    return jnp.dot(a, b, preferred_element_type=F32)


def head_blocks(rows, chans):
    row_head = lax.broadcasted_iota(jnp.int32, (rows, chans), 0) // TILE
    col_head = lax.broadcasted_iota(jnp.int32, (rows, chans), 1) // DH
    return row_head == col_head


def diagonal(full_t):
    parts = [full_t[h * DH : (h + 1) * DH, h * TILE : (h + 1) * TILE] for h in range(H)]
    return jnp.transpose(jnp.concatenate(parts, axis=0))


def attention_kernel(
    place_ref, mask_ref, x_ref, bias_ref, d_out_ref, w_proj_ref, w_out_ref,
    out_ref, dn_ref, pair_ref, bias_grad_ref,
    k_ref, v_ref, q_ref, do_ref, bias_f, grad_f, max_ref, sum_ref, delta_ref, acc_ref,
    gate_ref, dg_ref, list_ref,
):
    c = place_ref[0]
    tiles = 2 * x_ref.shape[0]
    rows = x_ref.shape[1]
    width = H * DH
    q_scale = DH ** (-0.5)
    query_tiles = (2 * c, tiles - 1 - 2 * c)
    w_q = w_proj_ref[:, :width]
    w_pair = w_proj_ref[:, width : 3 * width]
    w_gate = w_proj_ref[:, 3 * width :]

    def project(block, _):
        for r in range(rows):
            kv = nn(x_ref[block, r], w_pair).astype(BF16)
            for half in range(2):
                k_ref[2 * block + half, r] = kv[half * TILE : (half + 1) * TILE, :width]
                v_ref[2 * block + half, r] = kv[half * TILE : (half + 1) * TILE, width:]
        return 0

    lax.fori_loop(0, jnp.maximum(c, tiles // 2 - 1 - c) + 1, project, 0)

    counts, idles = [], []
    for a in range(2):
        def scan_tile(b, carried, a=a):
            count, idle = carried
            live = mask_ref[query_tiles[a], b] > 0
            list_ref[a, count] = b
            return jnp.where(live, count + 1, count), jnp.where(live, idle, b)

        count, idle = lax.fori_loop(0, tiles, scan_tile, (jnp.int32(0), jnp.int32(0)))
        for extra in range(CT):
            list_ref[a, count + extra] = query_tiles[a]
        counts.append(count)
        idles.append(idle)

    blocks = head_blocks(HJ, width)
    for a in range(2):
        tile = query_tiles[a]

        def prepare(r, _, a=a, tile=tile):
            x_q = x_ref[tile // 2, r, pl.ds(pl.multiple_of((tile % 2) * TILE, TILE), TILE), :]
            queries = (nn(x_q, w_q) * q_scale).astype(BF16)
            gating = jax.nn.sigmoid(nn(x_q, w_gate))
            d_gated = nt(d_out_ref[a, r], w_out_ref[...])
            d_att = (d_gated * gating).astype(BF16)
            zero = jnp.zeros((HJ, width), BF16)
            q_ref[a, r] = jnp.where(blocks, jnp.concatenate([queries] * H, axis=0), zero)
            do_ref[a, r] = jnp.where(blocks, jnp.concatenate([d_att] * H, axis=0), zero)
            gate_ref[a, r] = gating
            dg_ref[a, r] = d_gated
            return 0

        lax.fori_loop(0, rows, prepare, 0)

    def load_chunk(a, n):
        ids = [list_ref[a, n * CT + t] for t in range(CT)]
        for t in range(CT):
            block = bias_ref[a, ids[t]].astype(F32)
            shut = jnp.where(n * CT + t < counts[a], 0.0, neg_big)
            bias_f[t * TILE : (t + 1) * TILE, :] = block + shut
        return ids

    max_ref[...] = jnp.full(max_ref.shape, neg_big, F32)
    sum_ref[...] = jnp.zeros(sum_ref.shape, F32)
    acc_ref[...] = jnp.zeros(acc_ref.shape, F32)
    for a in range(2):
        def forward(n, _, a=a):
            ids = load_chunk(a, n)

            def per_row(r):
                keys = jnp.concatenate([k_ref[i, r] for i in ids], axis=0)
                values = jnp.concatenate([v_ref[i, r] for i in ids], axis=0)
                scores = nt(keys, q_ref[a, r]) + bias_f[...]
                old = max_ref[a, r]
                new = jnp.maximum(old, jnp.max(scores, axis=0, keepdims=True))
                fade = jnp.exp(old - new)
                probs = jnp.exp(scores - new)
                max_ref[a, r] = new
                sum_ref[a, r] = sum_ref[a, r] * fade + jnp.sum(probs, axis=0, keepdims=True)
                acc_ref[a, r] = acc_ref[a, r] * fade + tn(values, probs.astype(BF16))

            def some_rows(step, _):
                for u in range(2):
                    per_row(step * 2 + u)
                return 0

            lax.fori_loop(0, rows // 2, some_rows, 0)
            return 0

        lax.fori_loop(0, (counts[a] + CT - 1) // CT, forward, 0)

    for a in range(2):
        def middle(r, _, a=a):
            total = sum_ref[a, r]
            full_t = acc_ref[a, r] * (1.0 / total)
            max_ref[a, r] = max_ref[a, r] + jnp.log(total)
            delta_ref[a, r] = jnp.sum(
                full_t * jnp.transpose(do_ref[a, r].astype(F32)), axis=0, keepdims=True
            )
            attended = diagonal(full_t)
            gating = gate_ref[a, r]
            gated = (gating * attended).astype(BF16)
            out_ref[a, r] = nn(gated, w_out_ref[...]).astype(BF16)
            dg_ref[a, r] = dg_ref[a, r] * attended * gating * (1.0 - gating)
            acc_ref[a, r] = jnp.zeros(acc_ref.shape[2:], F32)
            return 0

        lax.fori_loop(0, rows, middle, 0)

    def clear(b, _):
        pair_ref[b] = jnp.zeros(pair_ref.shape[1:], BF16)
        for a in range(2):
            bias_grad_ref[a, b] = jnp.zeros(bias_grad_ref.shape[2:], BF16)
        return 0

    lax.fori_loop(0, tiles, clear, 0)
    for a in range(2):
        def backward(n, _, a=a):
            ids = load_chunk(a, n)

            def per_row(r, first):
                keys = jnp.concatenate([k_ref[i, r] for i in ids], axis=0)
                values = jnp.concatenate([v_ref[i, r] for i in ids], axis=0)
                q = q_ref[a, r]
                do = do_ref[a, r]
                probs = jnp.exp(nt(keys, q) + bias_f[...] - max_ref[a, r])
                d_scores = probs * (nt(values, do) - delta_ref[a, r])
                if first is None:
                    grad_f[...] += d_scores
                else:
                    grad_f[...] = jnp.where(first, d_scores, grad_f[...] + d_scores)
                d_b = d_scores.astype(BF16)
                acc_ref[a, r] += tn(keys, d_b)
                d_keys = nn(d_b, q)
                d_values = nn(probs.astype(BF16), do)
                both = jnp.concatenate([d_keys, d_values], axis=1).astype(BF16)
                term = nt(both, w_pair)
                for t in range(CT):
                    piece = term[t * TILE : (t + 1) * TILE]
                    pair_ref[ids[t], r] = (pair_ref[ids[t], r].astype(F32) + piece).astype(BF16)

            def some_rows(step, _):
                for u in range(2):
                    per_row(step * 2 + u, (step == 0) if u == 0 else None)
                return 0

            lax.fori_loop(0, rows // 2, some_rows, 0)
            for t in range(CT):
                target = jnp.where(n * CT + t < counts[a], ids[t], idles[a])
                bias_grad_ref[a, target] = grad_f[t * TILE : (t + 1) * TILE, :].astype(BF16)
            return 0

        lax.fori_loop(0, (counts[a] + CT - 1) // CT, backward, 0)

    for a in range(2):
        def finish(r, _, a=a):
            d_q = diagonal(acc_ref[a, r]) * q_scale
            d_q = nt(d_q.astype(BF16), w_q)
            dn_ref[a, r] = (d_q + nt(dg_ref[a, r].astype(BF16), w_gate)).astype(BF16)
            return 0

        lax.fori_loop(0, rows, finish, 0)


def attention(place, mask, x_all, bias_t, d_out, w_proj, w_out):
    blocks, rows, cols, chans = x_all.shape
    tiles = blocks * cols // TILE
    width = H * DH
    vmem = pl.BlockSpec(memory_space=pltpu.VMEM)
    smem = pl.BlockSpec(memory_space=pltpu.SMEM)
    return pl.pallas_call(
        attention_kernel,
        out_shape=(
            jax.ShapeDtypeStruct((2, rows, TILE, chans), BF16),
            jax.ShapeDtypeStruct((2, rows, TILE, chans), BF16),
            jax.ShapeDtypeStruct((tiles, rows, TILE, chans), BF16),
            jax.ShapeDtypeStruct((2, tiles, TILE, HJ), BF16),
        ),
        in_specs=[smem, smem, vmem, vmem, vmem, vmem, vmem],
        out_specs=(vmem,) * 4,
        scratch_shapes=[
            pltpu.VMEM((tiles, rows, TILE, width), BF16),
            pltpu.VMEM((tiles, rows, TILE, width), BF16),
            pltpu.VMEM((2, rows, HJ, width), BF16),
            pltpu.VMEM((2, rows, HJ, width), BF16),
            pltpu.VMEM((CT * TILE, HJ), F32),
            pltpu.VMEM((CT * TILE, HJ), F32),
            pltpu.VMEM((2, rows, 1, HJ), F32),
            pltpu.VMEM((2, rows, 1, HJ), F32),
            pltpu.VMEM((2, rows, 1, HJ), F32),
            pltpu.VMEM((2, rows, width, HJ), F32),
            pltpu.VMEM((2, rows, TILE, width), F32),
            pltpu.VMEM((2, rows, TILE, width), F32),
            pltpu.SMEM((2, tiles + CT), jnp.int32),
        ],
        compiler_params=pltpu.CompilerParams(vmem_limit_bytes=60 * 1024 * 1024),
        name="attention",
    )(place, mask, x_all, bias_t, d_out, w_proj, w_out)


MESH = pl.DeviceIdType.MESH
RING = 4


class Links:
    def __init__(self, send_sem, recv_sem):
        self.send_sem, self.recv_sem = send_sem, recv_sem
        self.count = 0
        self.sent = []

    def send(self, src, dst, device):
        n = self.count
        self.count += 1
        copy = pltpu.make_async_remote_copy(
            src_ref=src, dst_ref=dst, send_sem=self.send_sem.at[n], recv_sem=self.recv_sem.at[n],
            device_id=device, device_id_type=MESH,
        )
        copy.start()
        self.sent.append(copy)
        return n

    def arrived(self, n, dst):
        pltpu.make_async_remote_copy(
            src_ref=dst, dst_ref=dst, send_sem=self.send_sem.at[n], recv_sem=self.recv_sem.at[n],
            device_id=self.me, device_id_type=MESH,
        ).wait_recv()

    def finish(self):
        for copy in self.sent:
            copy.wait_send()


class Place:
    def __init__(self):
        self.row = lax.axis_index("row")
        self.col = lax.axis_index("col")
        self.core = self.col % 2
        z = (self.col // 2) % RING
        y = self.col // (2 * RING)
        self.yz = (y, z)

    def col_at(self, steps, core=None):
        y = (self.yz[0] + steps[0]) % RING
        z = (self.yz[1] + steps[1]) % RING
        return y * 2 * RING + z * 2 + (self.core if core is None else core)

    def along(self, axis, step):
        steps = [0, 0]
        steps[axis] = step
        return (self.row, self.col_at(steps))

    def along_x(self, step):
        return ((self.row + step) % RING, self.col)

    def sibling(self):
        return (self.row, self.col_at((0, 0), 1 - self.core))

    def partner(self):
        return (self.row, 8 * RING - 1 - self.col)


def greet(place):
    barrier = pltpu.get_barrier_semaphore()
    others = [place.along(axis, step) for axis in range(2) for step in (1, -1)]
    others += [place.along_x(1), place.along_x(-1), place.sibling(), place.partner()]
    for other in others:
        pl.semaphore_signal(barrier, inc=1, device_id=other, device_id_type=MESH)
    pl.semaphore_wait(barrier, len(others))


def pair_steps(axis, first, second):
    return (first, second) if axis == 0 else (second, first)


def gather_kernel(x_ref, bias_ref, d_ref, x_all, bias_all, d_odd, local_sem, send_sem, recv_sem):
    place = Place()
    links = Links(send_sem, recv_sem)
    links.me = place.sibling()
    greet(place)
    rows = x_ref.shape[0]
    half = rows // 2
    sub = half // 2
    long = bias_ref.shape[1]
    row = place.row

    def spot(steps, start, size, core=None):
        return x_all.at[place.col_at(steps, core), pl.ds(start, size)]

    def own(start, size):
        return x_ref.at[pl.ds(start, size)]

    def bias_spot(a, step, start=0, size=None):
        return bias_all.at[a, (row + step) % RING, pl.ds(start, long if size is None else size)]

    locals_ = [
        pltpu.make_async_copy(x_ref, x_all.at[place.col], local_sem.at[0]),
        pltpu.make_async_copy(bias_ref.at[0], bias_spot(0, 0), local_sem.at[1]),
    ]
    for copy in locals_:
        copy.start()

    odd = links.send(bias_ref.at[1], bias_spot(1, 0), place.partner())
    bias_direct = {}
    for step in (1, -1):
        bias_direct[0, step] = links.send(bias_ref.at[0], bias_spot(0, 0), place.along_x(step))
    first = {}
    for hf in range(2):
        mine = own(hf * half, half)
        for step in (1, -1):
            first[hf, step] = links.send(mine, spot((0, 0), hf * half, half), place.along(hf, step))
    second = {}
    chip = {}

    def pass_on(hf, offset, src=None):
        steps = pair_steps(hf, offset, 0)
        there = spot(steps, hf * half, half)
        for step in (1, -1):
            second[hf, offset, step] = links.send(there if src is None else src, there, place.along(1 - hf, step))
        chip[hf, offset, 0] = links.send(there if src is None else src, there, place.sibling())

    links.arrived(odd, bias_spot(1, 0))
    for step in (1, -1):
        bias_direct[1, step] = links.send(bias_spot(1, 0), bias_spot(1, 0), place.along_x(step))
    bias_onward = {}

    def bias_forward(a):
        for step in (1, -1):
            links.arrived(bias_direct[a, step], bias_spot(a, -step))
            piece = bias_spot(a, -step, 0 if step == 1 else long // 2, long // 2)
            bias_onward[a, step] = links.send(piece, piece, place.along_x(step))

    for hf in range(2):
        pass_on(hf, 0, own(hf * half, half))
    d_move = links.send(d_ref.at[1], d_odd, place.partner())

    onward = {}
    for step in (1, -1):
        for hf in range(2):
            links.arrived(first[hf, step], spot(pair_steps(hf, -step, 0), hf * half, half))
            begin = hf * half + (0 if step == 1 else sub)
            piece = spot(pair_steps(hf, -step, 0), begin, sub)
            onward[hf, step] = links.send(piece, piece, place.along(hf, step))
            pass_on(hf, -step)
    for hf in range(2):
        for step in (1, -1):
            begin = hf * half + (0 if step == 1 else sub)
            links.arrived(onward[hf, step], spot(pair_steps(hf, 2, 0), begin, sub))
        pass_on(hf, 2)

    far = {}
    for offset in (0, -1, 1, 2):
        for hf in range(2):
            for step in (1, -1):
                steps = pair_steps(hf, offset, -step)
                links.arrived(second[hf, offset, step], spot(steps, hf * half, half))
                begin = hf * half + (0 if step == 1 else sub)
                piece = spot(steps, begin, sub)
                far[hf, offset, step] = links.send(piece, piece, place.along(1 - hf, step))
                there = spot(steps, hf * half, half)
                chip[hf, offset, step] = links.send(there, there, place.sibling())
        if offset == 0:
            bias_forward(0)
        if offset == 1:
            bias_forward(1)
    for offset in (0, -1, 1, 2):
        for hf in range(2):
            steps = pair_steps(hf, offset, 2)
            for step in (1, -1):
                begin = hf * half + (0 if step == 1 else sub)
                links.arrived(far[hf, offset, step], spot(steps, begin, sub))
            there = spot(steps, hf * half, half)
            chip[hf, offset, 2] = links.send(there, there, place.sibling())
    for a in range(2):
        for step in (1, -1):
            begin = 0 if step == 1 else long // 2
            links.arrived(bias_onward[a, step], bias_spot(a, 2, begin, long // 2))
    links.arrived(d_move, d_odd)
    for (hf, offset, step), n in chip.items():
        steps = pair_steps(hf, offset, -step)
        links.arrived(n, spot(steps, hf * half, half, 1 - place.core))
    links.finish()
    for copy in locals_:
        copy.wait()


def gather(normed, bias_pair, d_out_pair):
    rows, cols, chans = normed.shape
    anywhere = pl.BlockSpec(memory_space=pl.ANY)
    copies = 100
    return pl.pallas_call(
        gather_kernel,
        out_shape=(
            jax.ShapeDtypeStruct((8 * RING, rows, cols, chans), BF16),
            jax.ShapeDtypeStruct((2, RING) + bias_pair.shape[1:], BF16),
            jax.ShapeDtypeStruct(d_out_pair.shape[1:], BF16),
        ),
        in_specs=[anywhere] * 3,
        out_specs=(anywhere,) * 3,
        scratch_shapes=[
            pltpu.SemaphoreType.DMA((2,)),
            pltpu.SemaphoreType.DMA((copies,)),
            pltpu.SemaphoreType.DMA((copies,)),
        ],
        compiler_params=pltpu.CompilerParams(collective_id=0, has_side_effects=True),
        name="gather",
    )(normed, bias_pair, d_out_pair)


def add_into(dst, *sources):
    def step(n, _):
        total = dst[n].astype(F32)
        for source in sources:
            total = total + source[n].astype(F32)
        dst[n] = total.astype(BF16)
        return 0

    lax.fori_loop(0, dst.shape[0], step, 0)


def reduce_kernel(
    pair_ref, grad_ref, out_ref, dn_ref, pair_sum, grad_all, out_odd, dn_odd,
    held, chip_in, one_in, two_in, last_one, last_two, grad_held, grad_one, grad_two,
    local_sem, send_sem, recv_sem, a2a_send, a2a_recv,
):
    place = Place()
    links = Links(send_sem, recv_sem)
    links.me = place.sibling()
    row, col = place.row, place.col
    ncol = grad_all.shape[1]
    rows = pair_ref.shape[2]
    sub = rows // 2
    groups = grad_held.shape[2]

    barrier = pltpu.get_barrier_semaphore()

    def greet_one(d, _):
        pl.semaphore_signal(barrier, inc=1, device_id=(row, (col + d) % ncol), device_id_type=MESH)
        return 0

    lax.fori_loop(1, ncol, greet_one, 0)
    for step in (1, -1):
        pl.semaphore_signal(barrier, inc=1, device_id=place.along_x(step), device_id_type=MESH)
    pl.semaphore_wait(barrier, ncol + 1)

    moves = [links.send(out_ref.at[1], out_odd, place.partner()), links.send(dn_ref.at[1], dn_odd, place.partner())]

    def half_of(step):
        return pl.ds(0 if step == 1 else groups // 2, groups // 2)

    grad_first = {}
    for a in range(2):
        for n, step in enumerate((1, -1)):
            grad_first[a, step] = links.send(
                grad_ref.at[a, (row + 2) % RING, half_of(step)], grad_one.at[a, n], place.along_x(step)
            )
    grad_local = {}
    for a in range(2):
        for rel in (1, 3, 0):
            n = len(grad_local)
            grad_local[a, rel] = pltpu.make_async_copy(
                grad_ref.at[a, (row + rel) % RING], grad_held.at[a, rel], local_sem.at[n]
            )
            grad_local[a, rel].start()

    def slot(hf, i, b):
        dy, dz = pair_steps(hf, i, b)
        return dy, dz, dy * RING + dz

    chip = {}
    local = {}
    for b in (2, 1, 3, 0):
        for hf in range(2):
            for i in (2, 1, 3, 0):
                dy, dz, n = slot(hf, i, b)
                chip[hf, i, b] = links.send(
                    pair_ref.at[place.col_at((dy, dz), 1 - place.core), hf], chip_in.at[n, hf], place.sibling()
                )
                local[hf, i, b] = pltpu.make_async_copy(
                    pair_ref.at[place.col_at((dy, dz)), hf], held.at[n, hf], local_sem.at[6 + len(local)]
                )
                local[hf, i, b].start()

    def collect(hf, i, b):
        n = slot(hf, i, b)[2]
        local[hf, i, b].wait()
        links.arrived(chip[hf, i, b], chip_in.at[n, hf])
        add_into(held.at[n, hf], chip_in.at[n, hf])
        return held.at[n, hf]

    def sub_of(step):
        return pl.ds(0 if step == 1 else sub, sub)

    one = {}
    for hf in range(2):
        for i in (2, 1, 3, 0):
            block = collect(hf, i, 2)
            for n, step in enumerate((1, -1)):
                one[hf, i, step] = links.send(
                    block.at[sub_of(step)], one_in.at[hf, i, n], place.along(1 - hf, step)
                )

    grad_second = {}
    for a in range(2):
        for n, step in enumerate((1, -1)):
            rel = step % RING
            grad_local[a, rel].wait()
            links.arrived(grad_first[a, step], grad_one.at[a, n])
            add_into(grad_held.at[a, rel, half_of(step)], grad_one.at[a, n])
            grad_second[a, step] = links.send(grad_held.at[a, rel], grad_two.at[a, n], place.along_x(step))

    two = {}
    for n, step in enumerate((1, -1)):
        for hf in range(2):
            for i in (2, 1, 3, 0):
                block = collect(hf, i, step % RING)
                links.arrived(one[hf, i, step], one_in.at[hf, i, n])
                add_into(block.at[sub_of(step)], one_in.at[hf, i, n])
                two[hf, i, step] = links.send(block, two_in.at[hf, i, n], place.along(1 - hf, step))
    mine = {(hf, i): collect(hf, i, 0) for hf in range(2) for i in (2, 1, 3, 0)}

    for a in range(2):
        grad_local[a, 0].wait()
        for n, step in enumerate((1, -1)):
            links.arrived(grad_second[a, step], grad_two.at[a, n])
        add_into(grad_held.at[a, 0], grad_two.at[a, 0], grad_two.at[a, 1])
    per = grad_all.shape[2]

    def keys_of(a, device):
        return grad_held.at[a, 0, pl.ds(device * per, per)]

    def a2a(a, d):
        target = (col + d) % ncol
        return pltpu.make_async_remote_copy(
            src_ref=keys_of(a, target), dst_ref=grad_all.at[a, col],
            send_sem=a2a_send.at[a, d], recv_sem=a2a_recv.at[a, d],
            device_id=(row, target), device_id_type=MESH,
        )

    def a2a_back(a, d):
        source = (col - d) % ncol
        return pltpu.make_async_remote_copy(
            src_ref=keys_of(a, source), dst_ref=grad_all.at[a, source],
            send_sem=a2a_send.at[a, d], recv_sem=a2a_recv.at[a, d],
            device_id=(row, source), device_id_type=MESH,
        )

    def a2a_start(d, _):
        for a in range(2):
            a2a(a, d).start()
        return 0

    lax.fori_loop(1, ncol, a2a_start, 0)
    keep = [pltpu.make_async_copy(keys_of(a, col), grad_all.at[a, col], local_sem.at[38 + a]) for a in range(2)]
    for copy in keep:
        copy.start()

    tail_one, tail_two = {}, {}
    for i in (2, 1, 3, 0):
        for hf in range(2):
            block = mine[hf, i]
            for n, step in enumerate((1, -1)):
                links.arrived(two[hf, i, step], two_in.at[hf, i, n])
            add_into(block, two_in.at[hf, i, 0], two_in.at[hf, i, 1])
            if i == 2:
                for n, step in enumerate((1, -1)):
                    tail_one[hf, step] = links.send(
                        block.at[sub_of(step)], last_one.at[hf, n], place.along(hf, step)
                    )
            elif i != 0:
                n, step = (0, 1) if i == 1 else (1, -1)
                links.arrived(tail_one[hf, step], last_one.at[hf, n])
                add_into(block.at[sub_of(step)], last_one.at[hf, n])
                tail_two[hf, step] = links.send(block, last_two.at[hf, n], place.along(hf, step))
    for hf in range(2):
        block = mine[hf, 0]
        for n, step in enumerate((1, -1)):
            links.arrived(tail_two[hf, step], last_two.at[hf, n])
        add_into(block, last_two.at[hf, 0], last_two.at[hf, 1])
        pair_sum[hf] = block[...]

    def a2a_end(d, _):
        for a in range(2):
            a2a_back(a, d).wait_recv()
            a2a(a, d).wait_send()
        return 0

    lax.fori_loop(1, ncol, a2a_end, 0)
    links.arrived(moves[0], out_odd)
    links.arrived(moves[1], dn_odd)
    links.finish()
    for copy in keep:
        copy.wait()


def reduce(pair, bias_grad, out, dn):
    ncol = 8 * RING
    rows, cols, chans = out.shape[1:]
    pair = pair.reshape(ncol, 2, rows, cols, chans)
    keys = bias_grad.shape[1] * TILE // RING
    unit = 32
    grads = bias_grad.reshape(2, RING, keys // unit, unit, HJ)
    part = keys // ncol
    anywhere = pl.BlockSpec(memory_space=pl.ANY)
    vmem = pl.BlockSpec(memory_space=pltpu.VMEM)
    block = (rows, cols, chans)
    half = (rows // 2, cols, chans)
    return pl.pallas_call(
        reduce_kernel,
        out_shape=(
            jax.ShapeDtypeStruct((2,) + block, BF16),
            jax.ShapeDtypeStruct((2, ncol, part // unit, unit, HJ), BF16),
            jax.ShapeDtypeStruct(block, BF16),
            jax.ShapeDtypeStruct(block, BF16),
        ),
        in_specs=[anywhere] * 4,
        out_specs=(vmem, anywhere, anywhere, anywhere),
        scratch_shapes=[
            pltpu.VMEM((RING * RING, 2) + block, BF16),
            pltpu.VMEM((RING * RING, 2) + block, BF16),
            pltpu.VMEM((2, RING, 2) + half, BF16),
            pltpu.VMEM((2, RING, 2) + block, BF16),
            pltpu.VMEM((2, 2) + half, BF16),
            pltpu.VMEM((2, 2) + block, BF16),
            pltpu.VMEM((2, RING, keys // unit, unit, HJ), BF16),
            pltpu.VMEM((2, 2, keys // unit // 2, unit, HJ), BF16),
            pltpu.VMEM((2, 2, keys // unit, unit, HJ), BF16),
            pltpu.SemaphoreType.DMA((40,)),
            pltpu.SemaphoreType.DMA((90,)),
            pltpu.SemaphoreType.DMA((90,)),
            pltpu.SemaphoreType.DMA((2, ncol)),
            pltpu.SemaphoreType.DMA((2, ncol)),
        ],
        compiler_params=pltpu.CompilerParams(
            collective_id=1, has_side_effects=True, vmem_limit_bytes=40 * 1024 * 1024
        ),
        name="reduce",
    )(pair, grads, out, dn)


def on_device(pair_slab, pair_bias, tile_mask, w_proj, w_out, d_out):
    rows, cols, chans = pair_slab.shape
    ncol = lax.axis_size("col")
    c = lax.axis_index("col")
    entries = pair_slab.astype(F32)
    centred = entries - jnp.mean(entries, axis=-1, keepdims=True)
    spread = jnp.mean(centred * centred, axis=-1, keepdims=True)
    rstd = lax.rsqrt(spread + eps_norm)
    normed_f = centred * rstd
    normed = normed_f.astype(BF16)

    halves = pair_bias.reshape(H, 2, TILE, -1).transpose(1, 3, 0, 2).reshape(2, -1, HJ)
    d_out_h = d_out.reshape(rows, 2, TILE, chans).transpose(1, 0, 2, 3)
    x_all, bias_all, d_odd = gather(normed, halves, d_out_h)
    bias_t = bias_all.reshape(2, -1, TILE, HJ)
    d_out_pair = jnp.stack([d_out_h[0], d_odd])

    out, dn, pair, bias_grad = attention(
        c.reshape(1).astype(jnp.int32), tile_mask, x_all, bias_t, d_out_pair, w_proj, w_out
    )

    pair_sum, grads, out_odd, dn_odd = reduce(pair, bias_grad, out, dn)
    attn_out = jnp.stack([out[0], out_odd], axis=1).reshape(rows, cols, chans)
    dn_own = jnp.stack([dn[0], dn_odd], axis=1).reshape(rows, cols, chans).astype(F32)
    pair_sum = pair_sum.transpose(1, 0, 2, 3).reshape(rows, cols, chans)
    d_normed = dn_own + pair_sum.astype(F32)
    slab_grads = rstd * (
        d_normed
        - jnp.mean(d_normed, axis=-1, keepdims=True)
        - normed_f * jnp.mean(d_normed * normed_f, axis=-1, keepdims=True)
    )
    grads = grads.reshape(2, ncol, -1, H, TILE)
    even = grads[0]
    odd = grads[1][::-1]
    both = jnp.stack([even, odd], axis=1).astype(F32)
    bias_grads = both.transpose(2, 3, 0, 1, 4).reshape(-1, H, ncol * cols)
    return attn_out, slab_grads.astype(BF16), bias_grads


def solution(mesh):
    in_specs = (P("row", "col", None), P(None, "col", "row"), P(), P(), P(), P("row", "col", None))
    out_specs = (P("row", "col", None), P("row", "col", None), P(("row", "col"), None, None))
    return jax.shard_map(
        on_device, mesh=mesh, in_specs=in_specs, out_specs=out_specs, check_vma=False
    )
```

```python
import functools

import jax
import jax.numpy as jnp
from jax import lax
from jax.experimental import pallas as pl
from jax.experimental.pallas import tpu as pltpu
from jax.sharding import PartitionSpec as P

H = 4
DH = 32
TILE = 64
HJ = H * TILE

eps_norm = 1e-05
neg_big = -1e30
CT = 8
GROUP = 8
SKEW = 2
F32 = jnp.float32
BF16 = jnp.bfloat16


def nt(a, b):
    return lax.dot_general(a, b, (((1,), (1,)), ((), ())), preferred_element_type=F32)


def tn(a, b):
    return lax.dot_general(a, b, (((0,), (0,)), ((), ())), preferred_element_type=F32)


def nn(a, b):
    return jnp.dot(a, b, preferred_element_type=F32)


def head_blocks(rows, chans):
    row_head = lax.broadcasted_iota(jnp.int32, (rows, chans), 0) // TILE
    col_head = lax.broadcasted_iota(jnp.int32, (rows, chans), 1) // DH
    return row_head == col_head


def diagonal(full_t):
    parts = [full_t[h * DH : (h + 1) * DH, h * TILE : (h + 1) * TILE] for h in range(H)]
    return jnp.transpose(jnp.concatenate(parts, axis=0))


def attention_kernel(
    place_ref, mask_ref, x_ref, bias_ref, d_out_ref, w_proj_ref, w_out_ref,
    out_ref, dn_ref, pair_ref, bias_grad_ref,
    k_ref, v_ref, q_ref, do_ref, bias_f, grad_f, max_ref, sum_ref, delta_ref, acc_ref,
    gate_ref, dg_ref, list_ref, qt_ref, dt_ref,
):
    c = place_ref[0]
    tiles = 2 * x_ref.shape[0]
    rows = x_ref.shape[1]
    width = H * DH
    q_scale = DH ** (-0.5)
    query_tiles = (2 * c, tiles - 1 - 2 * c)
    w_q = w_proj_ref[:, :width]
    w_pair = w_proj_ref[:, width : 3 * width]
    w_gate = w_proj_ref[:, 3 * width :]
    w_pair_t = jnp.transpose(w_pair)

    def project(block, _):
        kv = nn(x_ref[block].reshape(rows * 2 * TILE, -1), w_pair).astype(BF16)
        kv = kv.reshape(rows, 2 * TILE, 2 * width)
        for half in range(2):
            k_ref[2 * block + half] = kv[:, half * TILE : (half + 1) * TILE, :width]
            v_ref[2 * block + half] = kv[:, half * TILE : (half + 1) * TILE, width:]
        return 0

    lax.fori_loop(0, jnp.maximum(c, tiles // 2 - 1 - c) + 1, project, 0)

    counts, idles = [], []
    for a in range(2):
        def scan_tile(b, carried, a=a):
            count, idle = carried
            live = mask_ref[query_tiles[a], b] > 0
            list_ref[a, count] = b
            return jnp.where(live, count + 1, count), jnp.where(live, idle, b)

        count, idle = lax.fori_loop(0, tiles, scan_tile, (jnp.int32(0), jnp.int32(0)))
        for extra in range(CT):
            list_ref[a, count + extra] = query_tiles[a]
        counts.append(count)
        idles.append(idle)

    blocks = head_blocks(HJ, width)
    zero = jnp.zeros((HJ, width), BF16)
    for a in range(2):
        tile = query_tiles[a]
        x_q = x_ref[tile // 2, :, pl.ds(pl.multiple_of((tile % 2) * TILE, TILE), TILE), :]
        x_q = x_q.reshape(rows * TILE, -1)
        queries = (nn(x_q, w_q) * q_scale).astype(BF16)
        gating = jax.nn.sigmoid(nn(x_q, w_gate))
        d_gated = nt(d_out_ref[a].reshape(rows * TILE, -1), w_out_ref[...])
        d_att = (d_gated * gating).astype(BF16)
        gate_ref[a] = gating.reshape(rows, TILE, width)
        dg_ref[a] = d_gated.reshape(rows, TILE, width)
        for r in range(rows):
            part = slice(r * TILE, (r + 1) * TILE)
            q = jnp.where(blocks, jnp.concatenate([queries[part]] * H, axis=0), zero)
            do = jnp.where(blocks, jnp.concatenate([d_att[part]] * H, axis=0), zero)
            q_ref[a, r] = q
            do_ref[a, r] = do
            qt_ref[a, r] = jnp.transpose(q)
            dt_ref[a, r] = jnp.transpose(do)

    def load_chunk(a, n):
        ids = [list_ref[a, n * CT + t] for t in range(CT)]
        for t in range(CT):
            block = bias_ref[a, ids[t]].astype(F32)
            shut = jnp.where(n * CT + t < counts[a], 0.0, neg_big)
            bias_f[t * TILE : (t + 1) * TILE, :] = block + shut
        return ids

    max_ref[...] = jnp.full(max_ref.shape, neg_big, F32)
    sum_ref[...] = jnp.zeros(sum_ref.shape, F32)
    acc_ref[...] = jnp.zeros(acc_ref.shape, F32)
    for a in range(2):
        def forward(n, _, a=a):
            ids = load_chunk(a, n)

            def score(r):
                keys = jnp.concatenate([k_ref[i, r] for i in ids], axis=0)
                return nn(keys, qt_ref[a, r]) + bias_f[...]

            def use(r, scores):
                values = jnp.concatenate([v_ref[i, r] for i in ids], axis=0)
                old = max_ref[a, r]
                new = jnp.maximum(old, jnp.max(scores, axis=0, keepdims=True))
                fade = jnp.exp(old - new)
                probs = jnp.exp(scores - new)
                max_ref[a, r] = new
                sum_ref[a, r] = sum_ref[a, r] * fade + jnp.sum(probs, axis=0, keepdims=True)
                acc_ref[a, r] = acc_ref[a, r] * fade + tn(values, probs.astype(BF16))

            def some_rows(step, _):
                waiting = []
                for u in range(GROUP + SKEW):
                    if u < GROUP:
                        waiting.append(score(step * GROUP + u))
                    if u >= SKEW:
                        use(step * GROUP + u - SKEW, waiting.pop(0))
                return 0

            lax.fori_loop(0, rows // GROUP, some_rows, 0)
            return 0

        lax.fori_loop(0, (counts[a] + CT - 1) // CT, forward, 0)

    for a in range(2):
        attended = []
        for r in range(rows):
            total = sum_ref[a, r]
            full_t = acc_ref[a, r] * (1.0 / total)
            max_ref[a, r] = max_ref[a, r] + jnp.log(total)
            delta_ref[a, r] = jnp.sum(full_t * dt_ref[a, r].astype(F32), axis=0, keepdims=True)
            attended.append(diagonal(full_t))
            acc_ref[a, r] = jnp.zeros(acc_ref.shape[2:], F32)
        attended = jnp.concatenate(attended, axis=0).reshape(rows, TILE, width)
        gating = gate_ref[a]
        gated = (gating * attended).astype(BF16).reshape(rows * TILE, width)
        out_ref[a] = nn(gated, w_out_ref[...]).astype(BF16).reshape(rows, TILE, -1)
        dg_ref[a] = dg_ref[a] * attended * gating * (1.0 - gating)

    def clear(b, _):
        pair_ref[b] = jnp.zeros(pair_ref.shape[1:], BF16)
        for a in range(2):
            bias_grad_ref[a, b] = jnp.zeros(bias_grad_ref.shape[2:], BF16)
        return 0

    lax.fori_loop(0, tiles, clear, 0)
    for a in range(2):
        def backward(n, _, a=a):
            ids = load_chunk(a, n)

            def score(r):
                keys = jnp.concatenate([k_ref[i, r] for i in ids], axis=0)
                values = jnp.concatenate([v_ref[i, r] for i in ids], axis=0)
                return nn(keys, qt_ref[a, r]) + bias_f[...], nn(values, dt_ref[a, r])

            def use(r, made, first):
                scores, d_probs = made
                keys = jnp.concatenate([k_ref[i, r] for i in ids], axis=0)
                probs = jnp.exp(scores - max_ref[a, r])
                d_scores = probs * (d_probs - delta_ref[a, r])
                if first is None:
                    grad_f[...] += d_scores
                else:
                    grad_f[...] = jnp.where(first, d_scores, grad_f[...] + d_scores)
                d_b = d_scores.astype(BF16)
                acc_ref[a, r] += tn(keys, d_b)
                d_keys = nn(d_b, q_ref[a, r])
                d_values = nn(probs.astype(BF16), do_ref[a, r])
                both = jnp.concatenate([d_keys, d_values], axis=1).astype(BF16)
                term = nn(both, w_pair_t)
                for t in range(CT):
                    piece = term[t * TILE : (t + 1) * TILE]
                    pair_ref[ids[t], r] = (pair_ref[ids[t], r].astype(F32) + piece).astype(BF16)

            def some_rows(step, _):
                waiting = []
                for u in range(GROUP + SKEW):
                    if u < GROUP:
                        waiting.append(score(step * GROUP + u))
                    if u >= SKEW:
                        first = (step == 0) if u == SKEW else None
                        use(step * GROUP + u - SKEW, waiting.pop(0), first)
                return 0

            lax.fori_loop(0, rows // GROUP, some_rows, 0)
            for t in range(CT):
                target = jnp.where(n * CT + t < counts[a], ids[t], idles[a])
                bias_grad_ref[a, target] = grad_f[t * TILE : (t + 1) * TILE, :].astype(BF16)
            return 0

        lax.fori_loop(0, (counts[a] + CT - 1) // CT, backward, 0)

    for a in range(2):
        d_q = jnp.concatenate([diagonal(acc_ref[a, r]) for r in range(rows)], axis=0) * q_scale
        d_gate = dg_ref[a].reshape(rows * TILE, width)
        total = nt(d_q.astype(BF16), w_q) + nt(d_gate.astype(BF16), w_gate)
        dn_ref[a] = total.astype(BF16).reshape(rows, TILE, -1)


def attention(place, mask, x_all, bias_t, d_out, w_proj, w_out):
    blocks, rows, cols, chans = x_all.shape
    tiles = blocks * cols // TILE
    width = H * DH
    vmem = pl.BlockSpec(memory_space=pltpu.VMEM)
    smem = pl.BlockSpec(memory_space=pltpu.SMEM)
    return pl.pallas_call(
        attention_kernel,
        out_shape=(
            jax.ShapeDtypeStruct((2, rows, TILE, chans), BF16),
            jax.ShapeDtypeStruct((2, rows, TILE, chans), BF16),
            jax.ShapeDtypeStruct((tiles, rows, TILE, chans), BF16),
            jax.ShapeDtypeStruct((2, tiles, TILE, HJ), BF16),
        ),
        in_specs=[smem, smem, vmem, vmem, vmem, vmem, vmem],
        out_specs=(vmem,) * 4,
        scratch_shapes=[
            pltpu.VMEM((tiles, rows, TILE, width), BF16),
            pltpu.VMEM((tiles, rows, TILE, width), BF16),
            pltpu.VMEM((2, rows, HJ, width), BF16),
            pltpu.VMEM((2, rows, HJ, width), BF16),
            pltpu.VMEM((CT * TILE, HJ), F32),
            pltpu.VMEM((CT * TILE, HJ), F32),
            pltpu.VMEM((2, rows, 1, HJ), F32),
            pltpu.VMEM((2, rows, 1, HJ), F32),
            pltpu.VMEM((2, rows, 1, HJ), F32),
            pltpu.VMEM((2, rows, width, HJ), F32),
            pltpu.VMEM((2, rows, TILE, width), F32),
            pltpu.VMEM((2, rows, TILE, width), F32),
            pltpu.SMEM((2, tiles + CT), jnp.int32),
            pltpu.VMEM((2, rows, width, HJ), BF16),
            pltpu.VMEM((2, rows, width, HJ), BF16),
        ],
        compiler_params=pltpu.CompilerParams(vmem_limit_bytes=60 * 1024 * 1024),
        name="attention",
    )(place, mask, x_all, bias_t, d_out, w_proj, w_out)


MESH = pl.DeviceIdType.MESH
RING = 4


class Links:
    def __init__(self, send_sem, recv_sem):
        self.send_sem, self.recv_sem = send_sem, recv_sem
        self.count = 0
        self.sent = []

    def send(self, src, dst, device):
        n = self.count
        self.count += 1
        copy = pltpu.make_async_remote_copy(
            src_ref=src, dst_ref=dst, send_sem=self.send_sem.at[n], recv_sem=self.recv_sem.at[n],
            device_id=device, device_id_type=MESH,
        )
        copy.start()
        self.sent.append(copy)
        return n

    def arrived(self, n, dst):
        pltpu.make_async_remote_copy(
            src_ref=dst, dst_ref=dst, send_sem=self.send_sem.at[n], recv_sem=self.recv_sem.at[n],
            device_id=self.me, device_id_type=MESH,
        ).wait_recv()

    def finish(self):
        for copy in self.sent:
            copy.wait_send()


class Place:
    def __init__(self):
        self.row = lax.axis_index("row")
        self.col = lax.axis_index("col")
        self.core = self.col % 2
        z = (self.col // 2) % RING
        y = self.col // (2 * RING)
        self.yz = (y, z)

    def col_at(self, steps, core=None):
        y = (self.yz[0] + steps[0]) % RING
        z = (self.yz[1] + steps[1]) % RING
        return y * 2 * RING + z * 2 + (self.core if core is None else core)

    def along(self, axis, step):
        steps = [0, 0]
        steps[axis] = step
        return (self.row, self.col_at(steps))

    def along_x(self, step):
        return ((self.row + step) % RING, self.col)

    def sibling(self):
        return (self.row, self.col_at((0, 0), 1 - self.core))

    def partner(self):
        return (self.row, 8 * RING - 1 - self.col)


def greet(place):
    barrier = pltpu.get_barrier_semaphore()
    others = [place.along(axis, step) for axis in range(2) for step in (1, -1)]
    others += [place.along_x(1), place.along_x(-1), place.sibling(), place.partner()]
    for other in others:
        pl.semaphore_signal(barrier, inc=1, device_id=other, device_id_type=MESH)
    pl.semaphore_wait(barrier, len(others))


def pair_steps(axis, first, second):
    return (first, second) if axis == 0 else (second, first)


def gather_kernel(x_ref, bias_ref, d_ref, x_all, bias_all, d_odd, local_sem, send_sem, recv_sem):
    place = Place()
    links = Links(send_sem, recv_sem)
    links.me = place.sibling()
    greet(place)
    rows = x_ref.shape[0]
    half = rows // 2
    sub = half // 2
    long = bias_ref.shape[1]
    row = place.row

    def spot(steps, start, size, core=None):
        return x_all.at[place.col_at(steps, core), pl.ds(start, size)]

    def own(start, size):
        return x_ref.at[pl.ds(start, size)]

    def bias_spot(a, step, start=0, size=None):
        return bias_all.at[a, (row + step) % RING, pl.ds(start, long if size is None else size)]

    locals_ = [
        pltpu.make_async_copy(x_ref, x_all.at[place.col], local_sem.at[0]),
        pltpu.make_async_copy(bias_ref.at[0], bias_spot(0, 0), local_sem.at[1]),
    ]
    for copy in locals_:
        copy.start()

    odd = links.send(bias_ref.at[1], bias_spot(1, 0), place.partner())
    bias_direct = {}
    for step in (1, -1):
        bias_direct[0, step] = links.send(bias_ref.at[0], bias_spot(0, 0), place.along_x(step))
    first = {}
    for hf in range(2):
        mine = own(hf * half, half)
        for step in (1, -1):
            first[hf, step] = links.send(mine, spot((0, 0), hf * half, half), place.along(hf, step))
    second = {}
    chip = {}

    def pass_on(hf, offset, src=None):
        steps = pair_steps(hf, offset, 0)
        there = spot(steps, hf * half, half)
        for step in (1, -1):
            second[hf, offset, step] = links.send(there if src is None else src, there, place.along(1 - hf, step))
        chip[hf, offset, 0] = links.send(there if src is None else src, there, place.sibling())

    links.arrived(odd, bias_spot(1, 0))
    for step in (1, -1):
        bias_direct[1, step] = links.send(bias_spot(1, 0), bias_spot(1, 0), place.along_x(step))
    bias_onward = {}

    def bias_forward(a):
        for step in (1, -1):
            links.arrived(bias_direct[a, step], bias_spot(a, -step))
            piece = bias_spot(a, -step, 0 if step == 1 else long // 2, long // 2)
            bias_onward[a, step] = links.send(piece, piece, place.along_x(step))

    for hf in range(2):
        pass_on(hf, 0, own(hf * half, half))
    d_move = links.send(d_ref.at[1], d_odd, place.partner())

    onward = {}
    for step in (1, -1):
        for hf in range(2):
            links.arrived(first[hf, step], spot(pair_steps(hf, -step, 0), hf * half, half))
            begin = hf * half + (0 if step == 1 else sub)
            piece = spot(pair_steps(hf, -step, 0), begin, sub)
            onward[hf, step] = links.send(piece, piece, place.along(hf, step))
            pass_on(hf, -step)
    for hf in range(2):
        for step in (1, -1):
            begin = hf * half + (0 if step == 1 else sub)
            links.arrived(onward[hf, step], spot(pair_steps(hf, 2, 0), begin, sub))
        pass_on(hf, 2)

    far = {}
    for offset in (0, -1, 1, 2):
        for hf in range(2):
            for step in (1, -1):
                steps = pair_steps(hf, offset, -step)
                links.arrived(second[hf, offset, step], spot(steps, hf * half, half))
                begin = hf * half + (0 if step == 1 else sub)
                piece = spot(steps, begin, sub)
                far[hf, offset, step] = links.send(piece, piece, place.along(1 - hf, step))
                there = spot(steps, hf * half, half)
                chip[hf, offset, step] = links.send(there, there, place.sibling())
        if offset == 0:
            bias_forward(0)
        if offset == 1:
            bias_forward(1)
    for offset in (0, -1, 1, 2):
        for hf in range(2):
            steps = pair_steps(hf, offset, 2)
            for step in (1, -1):
                begin = hf * half + (0 if step == 1 else sub)
                links.arrived(far[hf, offset, step], spot(steps, begin, sub))
            there = spot(steps, hf * half, half)
            chip[hf, offset, 2] = links.send(there, there, place.sibling())
    for a in range(2):
        for step in (1, -1):
            begin = 0 if step == 1 else long // 2
            links.arrived(bias_onward[a, step], bias_spot(a, 2, begin, long // 2))
    links.arrived(d_move, d_odd)
    for (hf, offset, step), n in chip.items():
        steps = pair_steps(hf, offset, -step)
        links.arrived(n, spot(steps, hf * half, half, 1 - place.core))
    links.finish()
    for copy in locals_:
        copy.wait()


def gather(normed, bias_pair, d_out_pair):
    rows, cols, chans = normed.shape
    anywhere = pl.BlockSpec(memory_space=pl.ANY)
    copies = 100
    return pl.pallas_call(
        gather_kernel,
        out_shape=(
            jax.ShapeDtypeStruct((8 * RING, rows, cols, chans), BF16),
            jax.ShapeDtypeStruct((2, RING) + bias_pair.shape[1:], BF16),
            jax.ShapeDtypeStruct(d_out_pair.shape[1:], BF16),
        ),
        in_specs=[anywhere] * 3,
        out_specs=(anywhere,) * 3,
        scratch_shapes=[
            pltpu.SemaphoreType.DMA((2,)),
            pltpu.SemaphoreType.DMA((copies,)),
            pltpu.SemaphoreType.DMA((copies,)),
        ],
        compiler_params=pltpu.CompilerParams(collective_id=0, has_side_effects=True),
        name="gather",
    )(normed, bias_pair, d_out_pair)


def add_into(dst, *sources):
    def step(n, _):
        total = dst[n].astype(F32)
        for source in sources:
            total = total + source[n].astype(F32)
        dst[n] = total.astype(BF16)
        return 0

    lax.fori_loop(0, dst.shape[0], step, 0, unroll=4)


def reduce_kernel(
    pair_ref, grad_ref, out_ref, dn_ref, pair_sum, grad_all, out_odd, dn_odd,
    held, chip_in, one_in, two_in, last_one, last_two, grad_held, grad_one, grad_two,
    local_sem, send_sem, recv_sem, a2a_send, a2a_recv,
):
    place = Place()
    links = Links(send_sem, recv_sem)
    links.me = place.sibling()
    row, col = place.row, place.col
    ncol = grad_all.shape[1]
    rows = pair_ref.shape[2]
    sub = rows // 2
    groups = grad_held.shape[2]

    barrier = pltpu.get_barrier_semaphore()

    def greet_one(d, _):
        pl.semaphore_signal(barrier, inc=1, device_id=(row, (col + d) % ncol), device_id_type=MESH)
        return 0

    lax.fori_loop(1, ncol, greet_one, 0)
    for step in (1, -1):
        pl.semaphore_signal(barrier, inc=1, device_id=place.along_x(step), device_id_type=MESH)
    pl.semaphore_wait(barrier, ncol + 1)

    moves = [links.send(out_ref.at[1], out_odd, place.partner()), links.send(dn_ref.at[1], dn_odd, place.partner())]

    def half_of(step):
        return pl.ds(0 if step == 1 else groups // 2, groups // 2)

    grad_first = {}
    for a in range(2):
        for n, step in enumerate((1, -1)):
            grad_first[a, step] = links.send(
                grad_ref.at[a, (row + 2) % RING, half_of(step)], grad_one.at[a, n], place.along_x(step)
            )
    grad_local = {}
    for a in range(2):
        for rel in (1, 3, 0):
            n = len(grad_local)
            grad_local[a, rel] = pltpu.make_async_copy(
                grad_ref.at[a, (row + rel) % RING], grad_held.at[a, rel], local_sem.at[n]
            )
            grad_local[a, rel].start()

    def slot(hf, i, b):
        dy, dz = pair_steps(hf, i, b)
        return dy, dz, dy * RING + dz

    chip = {}
    local = {}
    for b in (2, 1, 3, 0):
        for hf in range(2):
            for i in (2, 1, 3, 0):
                dy, dz, n = slot(hf, i, b)
                chip[hf, i, b] = links.send(
                    pair_ref.at[place.col_at((dy, dz), 1 - place.core), hf], chip_in.at[n, hf], place.sibling()
                )
                local[hf, i, b] = pltpu.make_async_copy(
                    pair_ref.at[place.col_at((dy, dz)), hf], held.at[n, hf], local_sem.at[6 + len(local)]
                )
                local[hf, i, b].start()

    def collect(hf, i, b):
        n = slot(hf, i, b)[2]
        local[hf, i, b].wait()
        links.arrived(chip[hf, i, b], chip_in.at[n, hf])
        add_into(held.at[n, hf], chip_in.at[n, hf])
        return held.at[n, hf]

    def sub_of(step):
        return pl.ds(0 if step == 1 else sub, sub)

    one = {}
    for hf in range(2):
        for i in (2, 1, 3, 0):
            block = collect(hf, i, 2)
            for n, step in enumerate((1, -1)):
                one[hf, i, step] = links.send(
                    block.at[sub_of(step)], one_in.at[hf, i, n], place.along(1 - hf, step)
                )

    grad_second = {}
    for a in range(2):
        for n, step in enumerate((1, -1)):
            rel = step % RING
            grad_local[a, rel].wait()
            links.arrived(grad_first[a, step], grad_one.at[a, n])
            add_into(grad_held.at[a, rel, half_of(step)], grad_one.at[a, n])
            grad_second[a, step] = links.send(grad_held.at[a, rel], grad_two.at[a, n], place.along_x(step))

    two = {}
    for n, step in enumerate((1, -1)):
        for hf in range(2):
            for i in (2, 1, 3, 0):
                block = collect(hf, i, step % RING)
                links.arrived(one[hf, i, step], one_in.at[hf, i, n])
                add_into(block.at[sub_of(step)], one_in.at[hf, i, n])
                two[hf, i, step] = links.send(block, two_in.at[hf, i, n], place.along(1 - hf, step))
    mine = {(hf, i): collect(hf, i, 0) for hf in range(2) for i in (2, 1, 3, 0)}

    tail_one, tail_two = {}, {}
    for i in (2, 1, 3, 0):
        for hf in range(2):
            block = mine[hf, i]
            for n, step in enumerate((1, -1)):
                links.arrived(two[hf, i, step], two_in.at[hf, i, n])
            add_into(block, two_in.at[hf, i, 0], two_in.at[hf, i, 1])
            if i == 2:
                for n, step in enumerate((1, -1)):
                    tail_one[hf, step] = links.send(
                        block.at[sub_of(step)], last_one.at[hf, n], place.along(hf, step)
                    )
            elif i != 0:
                n, step = (0, 1) if i == 1 else (1, -1)
                links.arrived(tail_one[hf, step], last_one.at[hf, n])
                add_into(block.at[sub_of(step)], last_one.at[hf, n])
                tail_two[hf, step] = links.send(block, last_two.at[hf, n], place.along(hf, step))
    for a in range(2):
        grad_local[a, 0].wait()
        for n, step in enumerate((1, -1)):
            links.arrived(grad_second[a, step], grad_two.at[a, n])
        add_into(grad_held.at[a, 0], grad_two.at[a, 0], grad_two.at[a, 1])
    per = grad_all.shape[2]

    def keys_of(a, device):
        return grad_held.at[a, 0, pl.ds(device * per, per)]

    def a2a(a, d):
        target = (col + d) % ncol
        return pltpu.make_async_remote_copy(
            src_ref=keys_of(a, target), dst_ref=grad_all.at[a, col],
            send_sem=a2a_send.at[a, d], recv_sem=a2a_recv.at[a, d],
            device_id=(row, target), device_id_type=MESH,
        )

    def a2a_back(a, d):
        source = (col - d) % ncol
        return pltpu.make_async_remote_copy(
            src_ref=keys_of(a, source), dst_ref=grad_all.at[a, source],
            send_sem=a2a_send.at[a, d], recv_sem=a2a_recv.at[a, d],
            device_id=(row, source), device_id_type=MESH,
        )

    def a2a_start(d, _):
        for a in range(2):
            a2a(a, d).start()
        return 0

    lax.fori_loop(1, ncol, a2a_start, 0)
    keep = [pltpu.make_async_copy(keys_of(a, col), grad_all.at[a, col], local_sem.at[38 + a]) for a in range(2)]
    for copy in keep:
        copy.start()

    for hf in range(2):
        block = mine[hf, 0]
        for n, step in enumerate((1, -1)):
            links.arrived(tail_two[hf, step], last_two.at[hf, n])
        add_into(block, last_two.at[hf, 0], last_two.at[hf, 1])
        pair_sum[hf] = block[...]

    def a2a_end(d, _):
        for a in range(2):
            a2a_back(a, d).wait_recv()
            a2a(a, d).wait_send()
        return 0

    lax.fori_loop(1, ncol, a2a_end, 0)
    links.arrived(moves[0], out_odd)
    links.arrived(moves[1], dn_odd)
    links.finish()
    for copy in keep:
        copy.wait()


def reduce(pair, bias_grad, out, dn):
    ncol = 8 * RING
    rows, cols, chans = out.shape[1:]
    pair = pair.reshape(ncol, 2, rows, cols, chans)
    keys = bias_grad.shape[1] * TILE // RING
    unit = 32
    grads = bias_grad.reshape(2, RING, keys // unit, unit, HJ)
    part = keys // ncol
    anywhere = pl.BlockSpec(memory_space=pl.ANY)
    vmem = pl.BlockSpec(memory_space=pltpu.VMEM)
    block = (rows, cols, chans)
    half = (rows // 2, cols, chans)
    return pl.pallas_call(
        reduce_kernel,
        out_shape=(
            jax.ShapeDtypeStruct((2,) + block, BF16),
            jax.ShapeDtypeStruct((2, ncol, part // unit, unit, HJ), BF16),
            jax.ShapeDtypeStruct(block, BF16),
            jax.ShapeDtypeStruct(block, BF16),
        ),
        in_specs=[anywhere] * 4,
        out_specs=(vmem, anywhere, anywhere, anywhere),
        scratch_shapes=[
            pltpu.VMEM((RING * RING, 2) + block, BF16),
            pltpu.VMEM((RING * RING, 2) + block, BF16),
            pltpu.VMEM((2, RING, 2) + half, BF16),
            pltpu.VMEM((2, RING, 2) + block, BF16),
            pltpu.VMEM((2, 2) + half, BF16),
            pltpu.VMEM((2, 2) + block, BF16),
            pltpu.VMEM((2, RING, keys // unit, unit, HJ), BF16),
            pltpu.VMEM((2, 2, keys // unit // 2, unit, HJ), BF16),
            pltpu.VMEM((2, 2, keys // unit, unit, HJ), BF16),
            pltpu.SemaphoreType.DMA((40,)),
            pltpu.SemaphoreType.DMA((90,)),
            pltpu.SemaphoreType.DMA((90,)),
            pltpu.SemaphoreType.DMA((2, ncol)),
            pltpu.SemaphoreType.DMA((2, ncol)),
        ],
        compiler_params=pltpu.CompilerParams(
            collective_id=1, has_side_effects=True, vmem_limit_bytes=40 * 1024 * 1024
        ),
        name="reduce",
    )(pair, grads, out, dn)


def layout_kernel(grad_ref, out_ref):
    count = grad_ref.shape[1]
    for m in range(count):
        even = grad_ref[0, m].astype(F32)
        odd = grad_ref[1, count - 1 - m].astype(F32)
        for h in range(H):
            part = slice(h * TILE, (h + 1) * TILE)
            both = jnp.concatenate([even[:, part], odd[:, part]], axis=1)
            out_ref[:, h, 2 * TILE * m : 2 * TILE * (m + 1)] = both


def layout(grads):
    count, keys = grads.shape[1:3]
    vmem = pl.BlockSpec(memory_space=pltpu.VMEM)
    return pl.pallas_call(
        layout_kernel,
        out_shape=jax.ShapeDtypeStruct((keys, H, 2 * TILE * count), F32),
        in_specs=[vmem],
        out_specs=vmem,
        name="layout",
    )(grads)


def on_device(pair_slab, pair_bias, tile_mask, w_proj, w_out, d_out):
    rows, cols, chans = pair_slab.shape
    ncol = lax.axis_size("col")
    c = lax.axis_index("col")
    entries = pair_slab.astype(F32)
    centred = entries - jnp.mean(entries, axis=-1, keepdims=True)
    spread = jnp.mean(centred * centred, axis=-1, keepdims=True)
    rstd = lax.rsqrt(spread + eps_norm)
    normed_f = centred * rstd
    normed = normed_f.astype(BF16)

    halves = pair_bias.reshape(H, 2, TILE, -1).transpose(1, 3, 0, 2).reshape(2, -1, HJ)
    d_out_h = d_out.reshape(rows, 2, TILE, chans).transpose(1, 0, 2, 3)
    x_all, bias_all, d_odd = gather(normed, halves, d_out_h)
    bias_t = bias_all.reshape(2, -1, TILE, HJ)
    d_out_pair = jnp.stack([d_out_h[0], d_odd])

    out, dn, pair, bias_grad = attention(
        c.reshape(1).astype(jnp.int32), tile_mask, x_all, bias_t, d_out_pair, w_proj, w_out
    )

    pair_sum, grads, out_odd, dn_odd = reduce(pair, bias_grad, out, dn)
    attn_out = jnp.stack([out[0], out_odd], axis=1).reshape(rows, cols, chans)
    dn_own = jnp.stack([dn[0], dn_odd], axis=1).reshape(rows, cols, chans).astype(F32)
    pair_sum = pair_sum.transpose(1, 0, 2, 3).reshape(rows, cols, chans)
    d_normed = dn_own + pair_sum.astype(F32)
    slab_grads = rstd * (
        d_normed
        - jnp.mean(d_normed, axis=-1, keepdims=True)
        - normed_f * jnp.mean(d_normed * normed_f, axis=-1, keepdims=True)
    )
    bias_grads = layout(grads.reshape(2, ncol, -1, HJ))
    return attn_out, slab_grads.astype(BF16), bias_grads


def solution(mesh):
    in_specs = (P("row", "col", None), P(None, "col", "row"), P(), P(), P(), P("row", "col", None))
    out_specs = (P("row", "col", None), P("row", "col", None), P(("row", "col"), None, None))
    return jax.shard_map(
        on_device, mesh=mesh, in_specs=in_specs, out_specs=out_specs, check_vma=False
    )
```

```python
import functools

import jax
import jax.numpy as jnp
from jax import lax
from jax.experimental import pallas as pl
from jax.experimental.pallas import tpu as pltpu
from jax.sharding import PartitionSpec as P

H = 4
DH = 32
TILE = 64
HJ = H * TILE

eps_norm = 1e-05
neg_big = -1e30
CT = 8
GROUP = 8
SKEW = 2
F32 = jnp.float32
BF16 = jnp.bfloat16


def nt(a, b):
    return lax.dot_general(a, b, (((1,), (1,)), ((), ())), preferred_element_type=F32)


def tn(a, b):
    return lax.dot_general(a, b, (((0,), (0,)), ((), ())), preferred_element_type=F32)


def nn(a, b):
    return jnp.dot(a, b, preferred_element_type=F32)


def head_blocks(rows, chans):
    row_head = lax.broadcasted_iota(jnp.int32, (rows, chans), 0) // TILE
    col_head = lax.broadcasted_iota(jnp.int32, (rows, chans), 1) // DH
    return row_head == col_head


def diagonal(full_t):
    parts = [full_t[h * DH : (h + 1) * DH, h * TILE : (h + 1) * TILE] for h in range(H)]
    return jnp.transpose(jnp.concatenate(parts, axis=0))


def attention_kernel(
    place_ref, mask_ref, x_far, bias_far, d_out_ref, w_proj_ref, w_out_ref,
    out_ref, dn_ref, pair_far, bias_grad_far,
    x_ref, bias_ref, pair_ref, bias_grad_ref, x_sem, move_sem,
    k_ref, v_ref, q_ref, do_ref, bias_f, grad_f, max_ref, sum_ref, delta_ref, acc_ref,
    gate_ref, dg_ref, list_ref, qt_ref, dt_ref,
):
    c = place_ref[0]
    tiles = 2 * x_ref.shape[0]
    used = jnp.maximum(c, tiles // 2 - 1 - c) + 1

    def fetch(block):
        return pltpu.make_async_copy(x_far.at[block], x_ref.at[block], x_sem.at[block])

    def fetch_start(block, _):
        fetch(block).start()
        return 0

    lax.fori_loop(0, used, fetch_start, 0)
    bias_moves = [
        pltpu.make_async_copy(bias_far.at[a], bias_ref.at[a], move_sem.at[a]) for a in range(2)
    ]
    grad_moves = [
        pltpu.make_async_copy(bias_grad_ref.at[a], bias_grad_far.at[a], move_sem.at[2 + a]) for a in range(2)
    ]
    pair_move = pltpu.make_async_copy(pair_ref, pair_far, move_sem.at[4])
    for move in bias_moves:
        move.start()
    rows = x_ref.shape[1]
    width = H * DH
    q_scale = DH ** (-0.5)
    query_tiles = (2 * c, tiles - 1 - 2 * c)
    w_q = w_proj_ref[:, :width]
    w_pair = w_proj_ref[:, width : 3 * width]
    w_gate = w_proj_ref[:, 3 * width :]
    w_pair_t = jnp.transpose(w_pair)

    def clear(b, _):
        pair_ref[b] = jnp.zeros(pair_ref.shape[1:], BF16)
        for a in range(2):
            bias_grad_ref[a, b] = jnp.zeros(bias_grad_ref.shape[2:], BF16)
        return 0

    lax.fori_loop(0, tiles, clear, 0)

    def project(block, _):
        fetch(block).wait()
        kv = nn(x_ref[block].reshape(rows * 2 * TILE, -1), w_pair).astype(BF16)
        kv = kv.reshape(rows, 2 * TILE, 2 * width)
        for half in range(2):
            k_ref[2 * block + half] = kv[:, half * TILE : (half + 1) * TILE, :width]
            v_ref[2 * block + half] = kv[:, half * TILE : (half + 1) * TILE, width:]
        return 0

    lax.fori_loop(0, used, project, 0)

    counts, idles = [], []
    for a in range(2):
        def scan_tile(b, carried, a=a):
            count, idle = carried
            live = mask_ref[query_tiles[a], b] > 0
            list_ref[a, count] = b
            return jnp.where(live, count + 1, count), jnp.where(live, idle, b)

        count, idle = lax.fori_loop(0, tiles, scan_tile, (jnp.int32(0), jnp.int32(0)))
        for extra in range(CT):
            list_ref[a, count + extra] = query_tiles[a]
        counts.append(count)
        idles.append(idle)

    blocks = head_blocks(HJ, width)
    zero = jnp.zeros((HJ, width), BF16)
    for a in range(2):
        tile = query_tiles[a]
        x_q = x_ref[tile // 2, :, pl.ds(pl.multiple_of((tile % 2) * TILE, TILE), TILE), :]
        x_q = x_q.reshape(rows * TILE, -1)
        queries = (nn(x_q, w_q) * q_scale).astype(BF16)
        gating = jax.nn.sigmoid(nn(x_q, w_gate))
        d_gated = nt(d_out_ref[a].reshape(rows * TILE, -1), w_out_ref[...])
        d_att = (d_gated * gating).astype(BF16)
        gate_ref[a] = gating.reshape(rows, TILE, width)
        dg_ref[a] = d_gated.reshape(rows, TILE, width)
        for r in range(rows):
            part = slice(r * TILE, (r + 1) * TILE)
            q = jnp.where(blocks, jnp.concatenate([queries[part]] * H, axis=0), zero)
            do = jnp.where(blocks, jnp.concatenate([d_att[part]] * H, axis=0), zero)
            q_ref[a, r] = q
            do_ref[a, r] = do
            qt_ref[a, r] = jnp.transpose(q)
            dt_ref[a, r] = jnp.transpose(do)

    def load_chunk(a, start, ct):
        ids = [list_ref[a, start + t] for t in range(ct)]
        for t in range(ct):
            block = bias_ref[a, ids[t]].astype(F32)
            shut = jnp.where(start + t < counts[a], 0.0, neg_big)
            bias_f[t * TILE : (t + 1) * TILE, :] = block + shut
        return ids

    def walk(a, chunk):
        full = (counts[a] + CT // 2 - 1) // CT

        def step(n, _):
            chunk(a, n * CT, CT)
            return 0

        lax.fori_loop(0, full, step, 0)

        @pl.when(counts[a] > full * CT)
        def _():
            chunk(a, full * CT, CT // 2)

    max_ref[...] = jnp.full(max_ref.shape, neg_big, F32)
    sum_ref[...] = jnp.zeros(sum_ref.shape, F32)
    acc_ref[...] = jnp.zeros(acc_ref.shape, F32)
    def forward(a, start, ct):
        ids = load_chunk(a, start, ct)

        def score(r):
            keys = jnp.concatenate([k_ref[i, r] for i in ids], axis=0)
            return nn(keys, qt_ref[a, r]) + bias_f[: ct * TILE, :]

        def use(r, scores):
            values = jnp.concatenate([v_ref[i, r] for i in ids], axis=0)
            old = max_ref[a, r]
            new = jnp.maximum(old, jnp.max(scores, axis=0, keepdims=True))
            fade = jnp.exp(old - new)
            probs = jnp.exp(scores - new)
            max_ref[a, r] = new
            sum_ref[a, r] = sum_ref[a, r] * fade + jnp.sum(probs, axis=0, keepdims=True)
            acc_ref[a, r] = acc_ref[a, r] * fade + tn(values, probs.astype(BF16))

        def some_rows(step, _):
            waiting = []
            for u in range(GROUP + SKEW):
                if u < GROUP:
                    waiting.append(score(step * GROUP + u))
                if u >= SKEW:
                    use(step * GROUP + u - SKEW, waiting.pop(0))
            return 0

        lax.fori_loop(0, rows // GROUP, some_rows, 0)

    for a in range(2):
        bias_moves[a].wait()
        walk(a, forward)

    for a in range(2):
        attended = []
        for r in range(rows):
            total = sum_ref[a, r]
            full_t = acc_ref[a, r] * (1.0 / total)
            max_ref[a, r] = max_ref[a, r] + jnp.log(total)
            delta_ref[a, r] = jnp.sum(full_t * dt_ref[a, r].astype(F32), axis=0, keepdims=True)
            attended.append(diagonal(full_t))
            acc_ref[a, r] = jnp.zeros(acc_ref.shape[2:], F32)
        attended = jnp.concatenate(attended, axis=0).reshape(rows, TILE, width)
        gating = gate_ref[a]
        gated = (gating * attended).astype(BF16).reshape(rows * TILE, width)
        out_ref[a] = nn(gated, w_out_ref[...]).astype(BF16).reshape(rows, TILE, -1)
        dg_ref[a] = dg_ref[a] * attended * gating * (1.0 - gating)

    def backward(a, start, ct):
        ids = load_chunk(a, start, ct)

        def score(r):
            keys = jnp.concatenate([k_ref[i, r] for i in ids], axis=0)
            values = jnp.concatenate([v_ref[i, r] for i in ids], axis=0)
            return nn(keys, qt_ref[a, r]) + bias_f[: ct * TILE, :], nn(values, dt_ref[a, r])

        def use(r, made, first):
            scores, d_probs = made
            keys = jnp.concatenate([k_ref[i, r] for i in ids], axis=0)
            probs = jnp.exp(scores - max_ref[a, r])
            d_scores = probs * (d_probs - delta_ref[a, r])
            if first is None:
                grad_f[: ct * TILE, :] += d_scores
            else:
                grad_f[: ct * TILE, :] = jnp.where(first, d_scores, grad_f[: ct * TILE, :] + d_scores)
            d_b = d_scores.astype(BF16)
            acc_ref[a, r] += tn(keys, d_b)
            d_keys = nn(d_b, q_ref[a, r])
            d_values = nn(probs.astype(BF16), do_ref[a, r])
            both = jnp.concatenate([d_keys, d_values], axis=1).astype(BF16)
            term = nn(both, w_pair_t)
            for t in range(ct):
                piece = term[t * TILE : (t + 1) * TILE]
                pair_ref[ids[t], r] = (pair_ref[ids[t], r].astype(F32) + piece).astype(BF16)

        def some_rows(step, _):
            waiting = []
            for u in range(GROUP + SKEW):
                if u < GROUP:
                    waiting.append(score(step * GROUP + u))
                if u >= SKEW:
                    first = (step == 0) if u == SKEW else None
                    use(step * GROUP + u - SKEW, waiting.pop(0), first)
            return 0

        lax.fori_loop(0, rows // GROUP, some_rows, 0)
        for t in range(ct):
            target = jnp.where(start + t < counts[a], ids[t], idles[a])
            bias_grad_ref[a, target] = grad_f[t * TILE : (t + 1) * TILE, :].astype(BF16)

    for a in range(2):
        walk(a, backward)
        grad_moves[a].start()
    pair_move.start()

    for a in range(2):
        d_q = jnp.concatenate([diagonal(acc_ref[a, r]) for r in range(rows)], axis=0) * q_scale
        d_gate = dg_ref[a].reshape(rows * TILE, width)
        total = nt(d_q.astype(BF16), w_q) + nt(d_gate.astype(BF16), w_gate)
        dn_ref[a] = total.astype(BF16).reshape(rows, TILE, -1)
    for move in grad_moves + [pair_move]:
        move.wait()


def attention(place, mask, x_all, bias_t, d_out, w_proj, w_out):
    blocks, rows, cols, chans = x_all.shape
    tiles = blocks * cols // TILE
    width = H * DH
    vmem = pl.BlockSpec(memory_space=pltpu.VMEM)
    smem = pl.BlockSpec(memory_space=pltpu.SMEM)
    anywhere = pl.BlockSpec(memory_space=pl.ANY)
    return pl.pallas_call(
        attention_kernel,
        out_shape=(
            jax.ShapeDtypeStruct((2, rows, TILE, chans), BF16),
            jax.ShapeDtypeStruct((2, rows, TILE, chans), BF16),
            jax.ShapeDtypeStruct((tiles, rows, TILE, chans), BF16),
            jax.ShapeDtypeStruct((2, tiles, TILE, HJ), BF16),
        ),
        in_specs=[smem, smem, anywhere, anywhere, vmem, vmem, vmem],
        out_specs=(vmem, vmem, anywhere, anywhere),
        scratch_shapes=[
            pltpu.VMEM(x_all.shape, BF16),
            pltpu.VMEM(bias_t.shape, BF16),
            pltpu.VMEM((tiles, rows, TILE, chans), BF16),
            pltpu.VMEM((2, tiles, TILE, HJ), BF16),
            pltpu.SemaphoreType.DMA((blocks,)),
            pltpu.SemaphoreType.DMA((5,)),
            pltpu.VMEM((tiles, rows, TILE, width), BF16),
            pltpu.VMEM((tiles, rows, TILE, width), BF16),
            pltpu.VMEM((2, rows, HJ, width), BF16),
            pltpu.VMEM((2, rows, HJ, width), BF16),
            pltpu.VMEM((CT * TILE, HJ), F32),
            pltpu.VMEM((CT * TILE, HJ), F32),
            pltpu.VMEM((2, rows, 1, HJ), F32),
            pltpu.VMEM((2, rows, 1, HJ), F32),
            pltpu.VMEM((2, rows, 1, HJ), F32),
            pltpu.VMEM((2, rows, width, HJ), F32),
            pltpu.VMEM((2, rows, TILE, width), F32),
            pltpu.VMEM((2, rows, TILE, width), F32),
            pltpu.SMEM((2, tiles + CT), jnp.int32),
            pltpu.VMEM((2, rows, width, HJ), BF16),
            pltpu.VMEM((2, rows, width, HJ), BF16),
        ],
        compiler_params=pltpu.CompilerParams(vmem_limit_bytes=62 * 1024 * 1024),
        name="attention",
    )(place, mask, x_all, bias_t, d_out, w_proj, w_out)


MESH = pl.DeviceIdType.MESH
RING = 4


class Links:
    def __init__(self, send_sem, recv_sem):
        self.send_sem, self.recv_sem = send_sem, recv_sem
        self.count = 0
        self.sent = []

    def send(self, src, dst, device):
        n = self.count
        self.count += 1
        copy = pltpu.make_async_remote_copy(
            src_ref=src, dst_ref=dst, send_sem=self.send_sem.at[n], recv_sem=self.recv_sem.at[n],
            device_id=device, device_id_type=MESH,
        )
        copy.start()
        self.sent.append(copy)
        return n

    def arrived(self, n, dst):
        pltpu.make_async_remote_copy(
            src_ref=dst, dst_ref=dst, send_sem=self.send_sem.at[n], recv_sem=self.recv_sem.at[n],
            device_id=self.me, device_id_type=MESH,
        ).wait_recv()

    def finish(self):
        for copy in self.sent:
            copy.wait_send()


class Place:
    def __init__(self):
        self.row = lax.axis_index("row")
        self.col = lax.axis_index("col")
        self.core = self.col % 2
        z = (self.col // 2) % RING
        y = self.col // (2 * RING)
        self.yz = (y, z)

    def col_at(self, steps, core=None):
        y = (self.yz[0] + steps[0]) % RING
        z = (self.yz[1] + steps[1]) % RING
        return y * 2 * RING + z * 2 + (self.core if core is None else core)

    def along(self, axis, step):
        steps = [0, 0]
        steps[axis] = step
        return (self.row, self.col_at(steps))

    def along_x(self, step):
        return ((self.row + step) % RING, self.col)

    def sibling(self):
        return (self.row, self.col_at((0, 0), 1 - self.core))

    def partner(self):
        return (self.row, 8 * RING - 1 - self.col)


def greet(place):
    barrier = pltpu.get_barrier_semaphore()
    others = [place.along(axis, step) for axis in range(2) for step in (1, -1)]
    others += [place.along_x(1), place.along_x(-1), place.sibling(), place.partner()]
    for other in others:
        pl.semaphore_signal(barrier, inc=1, device_id=other, device_id_type=MESH)
    pl.semaphore_wait(barrier, len(others))


def pair_steps(axis, first, second):
    return (first, second) if axis == 0 else (second, first)


def gather_kernel(x_ref, bias_ref, d_ref, x_all, bias_all, d_odd, local_sem, send_sem, recv_sem):
    place = Place()
    links = Links(send_sem, recv_sem)
    links.me = place.sibling()
    greet(place)
    rows = x_ref.shape[0]
    half = rows // 2
    sub = half // 2
    long = bias_ref.shape[1]
    row = place.row

    def spot(steps, start, size, core=None):
        return x_all.at[place.col_at(steps, core), pl.ds(start, size)]

    def own(start, size):
        return x_ref.at[pl.ds(start, size)]

    def bias_spot(a, step, start=0, size=None):
        return bias_all.at[a, (row + step) % RING, pl.ds(start, long if size is None else size)]

    locals_ = [
        pltpu.make_async_copy(x_ref, x_all.at[place.col], local_sem.at[0]),
        pltpu.make_async_copy(bias_ref.at[0], bias_spot(0, 0), local_sem.at[1]),
    ]
    for copy in locals_:
        copy.start()

    odd = links.send(bias_ref.at[1], bias_spot(1, 0), place.partner())
    bias_direct = {}
    for step in (1, -1):
        bias_direct[0, step] = links.send(bias_ref.at[0], bias_spot(0, 0), place.along_x(step))
    first = {}
    for hf in range(2):
        mine = own(hf * half, half)
        for step in (1, -1):
            first[hf, step] = links.send(mine, spot((0, 0), hf * half, half), place.along(hf, step))
    second = {}
    chip = {}

    def pass_on(hf, offset, src=None):
        steps = pair_steps(hf, offset, 0)
        there = spot(steps, hf * half, half)
        for step in (1, -1):
            second[hf, offset, step] = links.send(there if src is None else src, there, place.along(1 - hf, step))
        chip[hf, offset, 0] = links.send(there if src is None else src, there, place.sibling())

    links.arrived(odd, bias_spot(1, 0))
    for step in (1, -1):
        bias_direct[1, step] = links.send(bias_spot(1, 0), bias_spot(1, 0), place.along_x(step))
    bias_onward = {}

    def bias_forward(a):
        for step in (1, -1):
            links.arrived(bias_direct[a, step], bias_spot(a, -step))
            piece = bias_spot(a, -step, 0 if step == 1 else long // 2, long // 2)
            bias_onward[a, step] = links.send(piece, piece, place.along_x(step))

    for hf in range(2):
        pass_on(hf, 0, own(hf * half, half))
    d_move = links.send(d_ref.at[1], d_odd, place.partner())

    onward = {}
    for step in (1, -1):
        for hf in range(2):
            links.arrived(first[hf, step], spot(pair_steps(hf, -step, 0), hf * half, half))
            begin = hf * half + (0 if step == 1 else sub)
            piece = spot(pair_steps(hf, -step, 0), begin, sub)
            onward[hf, step] = links.send(piece, piece, place.along(hf, step))
            pass_on(hf, -step)
    for hf in range(2):
        for step in (1, -1):
            begin = hf * half + (0 if step == 1 else sub)
            links.arrived(onward[hf, step], spot(pair_steps(hf, 2, 0), begin, sub))
        pass_on(hf, 2)

    far = {}
    for offset in (0, -1, 1, 2):
        for hf in range(2):
            for step in (1, -1):
                steps = pair_steps(hf, offset, -step)
                links.arrived(second[hf, offset, step], spot(steps, hf * half, half))
                begin = hf * half + (0 if step == 1 else sub)
                piece = spot(steps, begin, sub)
                far[hf, offset, step] = links.send(piece, piece, place.along(1 - hf, step))
                there = spot(steps, hf * half, half)
                chip[hf, offset, step] = links.send(there, there, place.sibling())
        if offset == 0:
            bias_forward(0)
        if offset == 1:
            bias_forward(1)
    for offset in (0, -1, 1, 2):
        for hf in range(2):
            steps = pair_steps(hf, offset, 2)
            for step in (1, -1):
                begin = hf * half + (0 if step == 1 else sub)
                links.arrived(far[hf, offset, step], spot(steps, begin, sub))
            there = spot(steps, hf * half, half)
            chip[hf, offset, 2] = links.send(there, there, place.sibling())
    for a in range(2):
        for step in (1, -1):
            begin = 0 if step == 1 else long // 2
            links.arrived(bias_onward[a, step], bias_spot(a, 2, begin, long // 2))
    links.arrived(d_move, d_odd)
    for (hf, offset, step), n in chip.items():
        steps = pair_steps(hf, offset, -step)
        links.arrived(n, spot(steps, hf * half, half, 1 - place.core))
    links.finish()
    for copy in locals_:
        copy.wait()


def gather(normed, bias_pair, d_out_pair):
    rows, cols, chans = normed.shape
    anywhere = pl.BlockSpec(memory_space=pl.ANY)
    copies = 100
    return pl.pallas_call(
        gather_kernel,
        out_shape=(
            jax.ShapeDtypeStruct((8 * RING, rows, cols, chans), BF16),
            jax.ShapeDtypeStruct((2, RING) + bias_pair.shape[1:], BF16),
            jax.ShapeDtypeStruct(d_out_pair.shape[1:], BF16),
        ),
        in_specs=[anywhere] * 3,
        out_specs=(anywhere,) * 3,
        scratch_shapes=[
            pltpu.SemaphoreType.DMA((2,)),
            pltpu.SemaphoreType.DMA((copies,)),
            pltpu.SemaphoreType.DMA((copies,)),
        ],
        compiler_params=pltpu.CompilerParams(collective_id=0, has_side_effects=True),
        name="gather",
    )(normed, bias_pair, d_out_pair)


def add_into(dst, *sources):
    def step(n, _):
        total = dst[n].astype(F32)
        for source in sources:
            total = total + source[n].astype(F32)
        dst[n] = total.astype(BF16)
        return 0

    lax.fori_loop(0, dst.shape[0], step, 0, unroll=4)


def reduce_kernel(
    pair_ref, grad_ref, out_ref, dn_ref, pair_sum, grad_all, out_odd, dn_odd,
    held, chip_in, one_in, two_in, last_one, last_two, grad_held, grad_one, grad_two,
    local_sem, send_sem, recv_sem, a2a_send, a2a_recv,
):
    place = Place()
    links = Links(send_sem, recv_sem)
    links.me = place.sibling()
    row, col = place.row, place.col
    ncol = grad_all.shape[1]
    rows = pair_ref.shape[2]
    sub = rows // 2
    groups = grad_held.shape[2]

    barrier = pltpu.get_barrier_semaphore()

    def greet_one(d, _):
        pl.semaphore_signal(barrier, inc=1, device_id=(row, (col + d) % ncol), device_id_type=MESH)
        return 0

    lax.fori_loop(1, ncol, greet_one, 0)
    for step in (1, -1):
        pl.semaphore_signal(barrier, inc=1, device_id=place.along_x(step), device_id_type=MESH)
    pl.semaphore_wait(barrier, ncol + 1)

    moves = [links.send(out_ref.at[1], out_odd, place.partner()), links.send(dn_ref.at[1], dn_odd, place.partner())]

    def half_of(step):
        return pl.ds(0 if step == 1 else groups // 2, groups // 2)

    grad_first = {}
    for a in range(2):
        for n, step in enumerate((1, -1)):
            grad_first[a, step] = links.send(
                grad_ref.at[a, (row + 2) % RING, half_of(step)], grad_one.at[a, n], place.along_x(step)
            )
    grad_local = {}
    for a in range(2):
        for rel in (1, 3, 0):
            n = len(grad_local)
            grad_local[a, rel] = pltpu.make_async_copy(
                grad_ref.at[a, (row + rel) % RING], grad_held.at[a, rel], local_sem.at[n]
            )
            grad_local[a, rel].start()

    def slot(hf, i, b):
        dy, dz = pair_steps(hf, i, b)
        return dy, dz, dy * RING + dz

    chip = {}
    local = {}
    for b in (2, 1, 3, 0):
        for hf in range(2):
            for i in (2, 1, 3, 0):
                dy, dz, n = slot(hf, i, b)
                chip[hf, i, b] = links.send(
                    pair_ref.at[place.col_at((dy, dz), 1 - place.core), hf], chip_in.at[n, hf], place.sibling()
                )
                local[hf, i, b] = pltpu.make_async_copy(
                    pair_ref.at[place.col_at((dy, dz)), hf], held.at[n, hf], local_sem.at[6 + len(local)]
                )
                local[hf, i, b].start()

    def collect(hf, i, b):
        n = slot(hf, i, b)[2]
        local[hf, i, b].wait()
        links.arrived(chip[hf, i, b], chip_in.at[n, hf])
        add_into(held.at[n, hf], chip_in.at[n, hf])
        return held.at[n, hf]

    def sub_of(step):
        return pl.ds(0 if step == 1 else sub, sub)

    one = {}
    for hf in range(2):
        for i in (2, 1, 3, 0):
            block = collect(hf, i, 2)
            for n, step in enumerate((1, -1)):
                one[hf, i, step] = links.send(
                    block.at[sub_of(step)], one_in.at[hf, i, n], place.along(1 - hf, step)
                )

    grad_second = {}
    for a in range(2):
        for n, step in enumerate((1, -1)):
            rel = step % RING
            grad_local[a, rel].wait()
            links.arrived(grad_first[a, step], grad_one.at[a, n])
            add_into(grad_held.at[a, rel, half_of(step)], grad_one.at[a, n])
            grad_second[a, step] = links.send(grad_held.at[a, rel], grad_two.at[a, n], place.along_x(step))

    two = {}
    for n, step in enumerate((1, -1)):
        for hf in range(2):
            for i in (2, 1, 3, 0):
                block = collect(hf, i, step % RING)
                links.arrived(one[hf, i, step], one_in.at[hf, i, n])
                add_into(block.at[sub_of(step)], one_in.at[hf, i, n])
                two[hf, i, step] = links.send(block, two_in.at[hf, i, n], place.along(1 - hf, step))
    mine = {(hf, i): collect(hf, i, 0) for hf in range(2) for i in (2, 1, 3, 0)}

    per = grad_all.shape[2]

    def keys_of(a, device):
        return grad_held.at[a, 0, pl.ds(device * per, per)]

    def a2a(a, d):
        target = (col + d) % ncol
        return pltpu.make_async_remote_copy(
            src_ref=keys_of(a, target), dst_ref=grad_all.at[a, col],
            send_sem=a2a_send.at[a, d], recv_sem=a2a_recv.at[a, d],
            device_id=(row, target), device_id_type=MESH,
        )

    def a2a_back(a, d):
        source = (col - d) % ncol
        return pltpu.make_async_remote_copy(
            src_ref=keys_of(a, source), dst_ref=grad_all.at[a, source],
            send_sem=a2a_send.at[a, d], recv_sem=a2a_recv.at[a, d],
            device_id=(row, source), device_id_type=MESH,
        )

    keep = []

    def finish_bias(a):
        grad_local[a, 0].wait()
        for n, step in enumerate((1, -1)):
            links.arrived(grad_second[a, step], grad_two.at[a, n])
        add_into(grad_held.at[a, 0], grad_two.at[a, 0], grad_two.at[a, 1])

        def start(d, _):
            a2a(a, d).start()
            return 0

        lax.fori_loop(1, ncol, start, 0)
        keep.append(pltpu.make_async_copy(keys_of(a, col), grad_all.at[a, col], local_sem.at[38 + a]))
        keep[-1].start()

    finish_bias(0)

    tail_one, tail_two = {}, {}
    for i in (2, 1, 3, 0):
        for hf in range(2):
            block = mine[hf, i]
            for n, step in enumerate((1, -1)):
                links.arrived(two[hf, i, step], two_in.at[hf, i, n])
            add_into(block, two_in.at[hf, i, 0], two_in.at[hf, i, 1])
            if i == 2:
                for n, step in enumerate((1, -1)):
                    tail_one[hf, step] = links.send(
                        block.at[sub_of(step)], last_one.at[hf, n], place.along(hf, step)
                    )
            elif i != 0:
                n, step = (0, 1) if i == 1 else (1, -1)
                links.arrived(tail_one[hf, step], last_one.at[hf, n])
                add_into(block.at[sub_of(step)], last_one.at[hf, n])
                tail_two[hf, step] = links.send(block, last_two.at[hf, n], place.along(hf, step))
    finish_bias(1)

    for hf in range(2):
        block = mine[hf, 0]
        for n, step in enumerate((1, -1)):
            links.arrived(tail_two[hf, step], last_two.at[hf, n])
        add_into(block, last_two.at[hf, 0], last_two.at[hf, 1])
        pair_sum[hf] = block[...]

    def a2a_end(d, _):
        for a in range(2):
            a2a_back(a, d).wait_recv()
            a2a(a, d).wait_send()
        return 0

    lax.fori_loop(1, ncol, a2a_end, 0)
    links.arrived(moves[0], out_odd)
    links.arrived(moves[1], dn_odd)
    links.finish()
    for copy in keep:
        copy.wait()


def reduce(pair, bias_grad, out, dn):
    ncol = 8 * RING
    rows, cols, chans = out.shape[1:]
    pair = pair.reshape(ncol, 2, rows, cols, chans)
    keys = bias_grad.shape[1] * TILE // RING
    unit = 32
    grads = bias_grad.reshape(2, RING, keys // unit, unit, HJ)
    part = keys // ncol
    anywhere = pl.BlockSpec(memory_space=pl.ANY)
    vmem = pl.BlockSpec(memory_space=pltpu.VMEM)
    block = (rows, cols, chans)
    half = (rows // 2, cols, chans)
    return pl.pallas_call(
        reduce_kernel,
        out_shape=(
            jax.ShapeDtypeStruct((2,) + block, BF16),
            jax.ShapeDtypeStruct((2, ncol, part // unit, unit, HJ), BF16),
            jax.ShapeDtypeStruct(block, BF16),
            jax.ShapeDtypeStruct(block, BF16),
        ),
        in_specs=[anywhere] * 4,
        out_specs=(vmem, anywhere, anywhere, anywhere),
        scratch_shapes=[
            pltpu.VMEM((RING * RING, 2) + block, BF16),
            pltpu.VMEM((RING * RING, 2) + block, BF16),
            pltpu.VMEM((2, RING, 2) + half, BF16),
            pltpu.VMEM((2, RING, 2) + block, BF16),
            pltpu.VMEM((2, 2) + half, BF16),
            pltpu.VMEM((2, 2) + block, BF16),
            pltpu.VMEM((2, RING, keys // unit, unit, HJ), BF16),
            pltpu.VMEM((2, 2, keys // unit // 2, unit, HJ), BF16),
            pltpu.VMEM((2, 2, keys // unit, unit, HJ), BF16),
            pltpu.SemaphoreType.DMA((40,)),
            pltpu.SemaphoreType.DMA((90,)),
            pltpu.SemaphoreType.DMA((90,)),
            pltpu.SemaphoreType.DMA((2, ncol)),
            pltpu.SemaphoreType.DMA((2, ncol)),
        ],
        compiler_params=pltpu.CompilerParams(
            collective_id=1, has_side_effects=True, vmem_limit_bytes=62 * 1024 * 1024
        ),
        name="reduce",
    )(pair, grads, out, dn)


def layout_kernel(grad_ref, out_ref):
    count = grad_ref.shape[1]
    for m in range(count):
        even = grad_ref[0, m].astype(F32)
        odd = grad_ref[1, count - 1 - m].astype(F32)
        for h in range(H):
            part = slice(h * TILE, (h + 1) * TILE)
            both = jnp.concatenate([even[:, part], odd[:, part]], axis=1)
            out_ref[:, h, 2 * TILE * m : 2 * TILE * (m + 1)] = both


def layout(grads):
    count, keys = grads.shape[1:3]
    vmem = pl.BlockSpec(memory_space=pltpu.VMEM)
    return pl.pallas_call(
        layout_kernel,
        out_shape=jax.ShapeDtypeStruct((keys, H, 2 * TILE * count), F32),
        in_specs=[vmem],
        out_specs=vmem,
        name="layout",
    )(grads)


def on_device(pair_slab, pair_bias, tile_mask, w_proj, w_out, d_out):
    rows, cols, chans = pair_slab.shape
    ncol = lax.axis_size("col")
    c = lax.axis_index("col")
    entries = pair_slab.astype(F32)
    centred = entries - jnp.mean(entries, axis=-1, keepdims=True)
    spread = jnp.mean(centred * centred, axis=-1, keepdims=True)
    rstd = lax.rsqrt(spread + eps_norm)
    normed_f = centred * rstd
    normed = normed_f.astype(BF16)

    halves = pair_bias.reshape(H, 2, TILE, -1).transpose(1, 3, 0, 2).reshape(2, -1, HJ)
    d_out_h = d_out.reshape(rows, 2, TILE, chans).transpose(1, 0, 2, 3)
    x_all, bias_all, d_odd = gather(normed, halves, d_out_h)
    bias_t = bias_all.reshape(2, -1, TILE, HJ)
    d_out_pair = jnp.stack([d_out_h[0], d_odd])

    out, dn, pair, bias_grad = attention(
        c.reshape(1).astype(jnp.int32), tile_mask, x_all, bias_t, d_out_pair, w_proj, w_out
    )

    pair_sum, grads, out_odd, dn_odd = reduce(pair, bias_grad, out, dn)
    attn_out = jnp.stack([out[0], out_odd], axis=1).reshape(rows, cols, chans)
    dn_own = jnp.stack([dn[0], dn_odd], axis=1).reshape(rows, cols, chans).astype(F32)
    pair_sum = pair_sum.transpose(1, 0, 2, 3).reshape(rows, cols, chans)
    d_normed = dn_own + pair_sum.astype(F32)
    slab_grads = rstd * (
        d_normed
        - jnp.mean(d_normed, axis=-1, keepdims=True)
        - normed_f * jnp.mean(d_normed * normed_f, axis=-1, keepdims=True)
    )
    bias_grads = layout(grads.reshape(2, ncol, -1, HJ))
    return attn_out, slab_grads.astype(BF16), bias_grads


def solution(mesh):
    in_specs = (P("row", "col", None), P(None, "col", "row"), P(), P(), P(), P("row", "col", None))
    out_specs = (P("row", "col", None), P("row", "col", None), P(("row", "col"), None, None))
    return jax.shard_map(
        on_device, mesh=mesh, in_specs=in_specs, out_specs=out_specs, check_vma=False
    )
```

```python
import functools

import jax
import jax.numpy as jnp
from jax import lax
from jax.experimental import pallas as pl
from jax.experimental.pallas import tpu as pltpu
from jax.sharding import PartitionSpec as P

H = 4
DH = 32
TILE = 64
HJ = H * TILE

eps_norm = 1e-05
neg_big = -1e30
CT = 8
GROUP = 8
SKEW = 2
F32 = jnp.float32
BF16 = jnp.bfloat16


def nt(a, b):
    return lax.dot_general(a, b, (((1,), (1,)), ((), ())), preferred_element_type=F32)


def tn(a, b):
    return lax.dot_general(a, b, (((0,), (0,)), ((), ())), preferred_element_type=F32)


def nn(a, b):
    return jnp.dot(a, b, preferred_element_type=F32)


def head_blocks(rows, chans):
    row_head = lax.broadcasted_iota(jnp.int32, (rows, chans), 0) // TILE
    col_head = lax.broadcasted_iota(jnp.int32, (rows, chans), 1) // DH
    return row_head == col_head


def diagonal(full_t):
    parts = [full_t[h * DH : (h + 1) * DH, h * TILE : (h + 1) * TILE] for h in range(H)]
    return jnp.transpose(jnp.concatenate(parts, axis=0))


def attention_kernel(
    place_ref, mask_ref, x_far, bias_far, d_out_ref, d_odd_ref, w_proj_ref, w_out_ref,
    out_ref, dn_ref, pair_far, bias_grad_far,
    x_ref, bias_ref, pair_ref, bias_grad_ref, x_sem, move_sem,
    k_ref, v_ref, q_ref, do_ref, bias_f, grad_f, max_ref, sum_ref, delta_ref, acc_ref,
    gate_ref, dg_ref, list_ref, qt_ref, dt_ref,
):
    c = place_ref[0]
    tiles = 2 * x_ref.shape[0]
    used = jnp.maximum(c, tiles // 2 - 1 - c) + 1

    def fetch(block):
        return pltpu.make_async_copy(x_far.at[block], x_ref.at[block], x_sem.at[block])

    def fetch_start(block, _):
        fetch(block).start()
        return 0

    lax.fori_loop(0, used, fetch_start, 0)
    bias_moves = [
        pltpu.make_async_copy(bias_far.at[a], bias_ref.at[a], move_sem.at[a]) for a in range(2)
    ]
    grad_moves = [
        pltpu.make_async_copy(bias_grad_ref.at[a], bias_grad_far.at[a], move_sem.at[2 + a]) for a in range(2)
    ]
    pair_move = pltpu.make_async_copy(pair_ref, pair_far, move_sem.at[4])
    for move in bias_moves:
        move.start()
    rows = x_ref.shape[1]
    width = H * DH
    q_scale = DH ** (-0.5)
    query_tiles = (2 * c, tiles - 1 - 2 * c)
    w_q = w_proj_ref[:, :width]
    w_pair = w_proj_ref[:, width : 3 * width]
    w_gate = w_proj_ref[:, 3 * width :]
    w_pair_t = jnp.transpose(w_pair)

    def clear(b, _):
        pair_ref[b] = jnp.zeros(pair_ref.shape[1:], BF16)
        for a in range(2):
            bias_grad_ref[a, b] = jnp.zeros(bias_grad_ref.shape[2:], BF16)
        return 0

    lax.fori_loop(0, tiles, clear, 0)

    def project(block, _):
        fetch(block).wait()
        kv = nn(x_ref[block].reshape(rows * 2 * TILE, -1), w_pair).astype(BF16)
        kv = kv.reshape(rows, 2 * TILE, 2 * width)
        for half in range(2):
            k_ref[2 * block + half] = kv[:, half * TILE : (half + 1) * TILE, :width]
            v_ref[2 * block + half] = kv[:, half * TILE : (half + 1) * TILE, width:]
        return 0

    lax.fori_loop(0, used, project, 0)

    counts, idles = [], []
    for a in range(2):
        def scan_tile(b, carried, a=a):
            count, idle = carried
            live = mask_ref[query_tiles[a], b] > 0
            list_ref[a, count] = b
            return jnp.where(live, count + 1, count), jnp.where(live, idle, b)

        count, idle = lax.fori_loop(0, tiles, scan_tile, (jnp.int32(0), jnp.int32(0)))
        for extra in range(CT):
            list_ref[a, count + extra] = query_tiles[a]
        counts.append(count)
        idles.append(idle)

    blocks = head_blocks(HJ, width)
    zero = jnp.zeros((HJ, width), BF16)
    for a in range(2):
        tile = query_tiles[a]
        x_q = x_ref[tile // 2, :, pl.ds(pl.multiple_of((tile % 2) * TILE, TILE), TILE), :]
        x_q = x_q.reshape(rows * TILE, -1)
        queries = (nn(x_q, w_q) * q_scale).astype(BF16)
        gating = jax.nn.sigmoid(nn(x_q, w_gate))
        d_out = d_out_ref[:, :TILE] if a == 0 else d_odd_ref[...]
        d_gated = nt(d_out.reshape(rows * TILE, -1), w_out_ref[...])
        d_att = (d_gated * gating).astype(BF16)
        gate_ref[a] = gating.reshape(rows, TILE, width)
        dg_ref[a] = d_gated.reshape(rows, TILE, width)
        for r in range(rows):
            part = slice(r * TILE, (r + 1) * TILE)
            q = jnp.where(blocks, jnp.concatenate([queries[part]] * H, axis=0), zero)
            do = jnp.where(blocks, jnp.concatenate([d_att[part]] * H, axis=0), zero)
            q_ref[a, r] = q
            do_ref[a, r] = do
            qt_ref[a, r] = jnp.transpose(q)
            dt_ref[a, r] = jnp.transpose(do)

    def load_chunk(a, start, ct):
        ids = [list_ref[a, start + t] for t in range(ct)]
        for t in range(ct):
            block = bias_ref[a, ids[t]].astype(F32)
            shut = jnp.where(start + t < counts[a], 0.0, neg_big)
            bias_f[t * TILE : (t + 1) * TILE, :] = block + shut
        return ids

    def walk(a, chunk):
        full = (counts[a] + CT // 2 - 1) // CT

        def step(n, _):
            chunk(a, n * CT, CT)
            return 0

        lax.fori_loop(0, full, step, 0)

        @pl.when(counts[a] > full * CT)
        def _():
            chunk(a, full * CT, CT // 2)

    max_ref[...] = jnp.full(max_ref.shape, neg_big, F32)
    sum_ref[...] = jnp.zeros(sum_ref.shape, F32)
    acc_ref[...] = jnp.zeros(acc_ref.shape, F32)
    def forward(a, start, ct):
        ids = load_chunk(a, start, ct)

        def score(r):
            keys = jnp.concatenate([k_ref[i, r] for i in ids], axis=0)
            return nn(keys, qt_ref[a, r]) + bias_f[: ct * TILE, :]

        def use(r, scores):
            values = jnp.concatenate([v_ref[i, r] for i in ids], axis=0)
            old = max_ref[a, r]
            new = jnp.maximum(old, jnp.max(scores, axis=0, keepdims=True))
            fade = jnp.exp(old - new)
            probs = jnp.exp(scores - new)
            max_ref[a, r] = new
            sum_ref[a, r] = sum_ref[a, r] * fade + jnp.sum(probs, axis=0, keepdims=True)
            acc_ref[a, r] = acc_ref[a, r] * fade + tn(values, probs.astype(BF16))

        def some_rows(step, _):
            waiting = []
            for u in range(GROUP + SKEW):
                if u < GROUP:
                    waiting.append(score(step * GROUP + u))
                if u >= SKEW:
                    use(step * GROUP + u - SKEW, waiting.pop(0))
            return 0

        lax.fori_loop(0, rows // GROUP, some_rows, 0)

    for a in range(2):
        bias_moves[a].wait()
        walk(a, forward)

    for a in range(2):
        attended = []
        for r in range(rows):
            total = sum_ref[a, r]
            full_t = acc_ref[a, r] * (1.0 / total)
            max_ref[a, r] = max_ref[a, r] + jnp.log(total)
            delta_ref[a, r] = jnp.sum(full_t * dt_ref[a, r].astype(F32), axis=0, keepdims=True)
            attended.append(diagonal(full_t))
            acc_ref[a, r] = jnp.zeros(acc_ref.shape[2:], F32)
        attended = jnp.concatenate(attended, axis=0).reshape(rows, TILE, width)
        gating = gate_ref[a]
        gated = (gating * attended).astype(BF16).reshape(rows * TILE, width)
        out_ref[a] = nn(gated, w_out_ref[...]).astype(BF16).reshape(rows, TILE, -1)
        dg_ref[a] = dg_ref[a] * attended * gating * (1.0 - gating)

    def backward(a, start, ct):
        ids = load_chunk(a, start, ct)

        def score(r):
            keys = jnp.concatenate([k_ref[i, r] for i in ids], axis=0)
            values = jnp.concatenate([v_ref[i, r] for i in ids], axis=0)
            return nn(keys, qt_ref[a, r]) + bias_f[: ct * TILE, :], nn(values, dt_ref[a, r])

        def use(r, made, first):
            scores, d_probs = made
            keys = jnp.concatenate([k_ref[i, r] for i in ids], axis=0)
            probs = jnp.exp(scores - max_ref[a, r])
            d_scores = probs * (d_probs - delta_ref[a, r])
            if first is None:
                grad_f[: ct * TILE, :] += d_scores
            else:
                grad_f[: ct * TILE, :] = jnp.where(first, d_scores, grad_f[: ct * TILE, :] + d_scores)
            d_b = d_scores.astype(BF16)
            acc_ref[a, r] += tn(keys, d_b)
            d_keys = nn(d_b, q_ref[a, r])
            d_values = nn(probs.astype(BF16), do_ref[a, r])
            both = jnp.concatenate([d_keys, d_values], axis=1).astype(BF16)
            term = nn(both, w_pair_t)
            for t in range(ct):
                piece = term[t * TILE : (t + 1) * TILE]
                pair_ref[ids[t], r] = (pair_ref[ids[t], r].astype(F32) + piece).astype(BF16)

        def some_rows(step, _):
            waiting = []
            for u in range(GROUP + SKEW):
                if u < GROUP:
                    waiting.append(score(step * GROUP + u))
                if u >= SKEW:
                    first = (step == 0) if u == SKEW else None
                    use(step * GROUP + u - SKEW, waiting.pop(0), first)
            return 0

        lax.fori_loop(0, rows // GROUP, some_rows, 0)
        for t in range(ct):
            target = jnp.where(start + t < counts[a], ids[t], idles[a])
            bias_grad_ref[a, target] = grad_f[t * TILE : (t + 1) * TILE, :].astype(BF16)

    for a in range(2):
        walk(a, backward)
        grad_moves[a].start()
    pair_move.start()

    for a in range(2):
        d_q = jnp.concatenate([diagonal(acc_ref[a, r]) for r in range(rows)], axis=0) * q_scale
        d_gate = dg_ref[a].reshape(rows * TILE, width)
        total = nt(d_q.astype(BF16), w_q) + nt(d_gate.astype(BF16), w_gate)
        dn_ref[a] = total.astype(BF16).reshape(rows, TILE, -1)
    for move in grad_moves + [pair_move]:
        move.wait()


def attention(place, mask, x_all, bias_t, d_out, d_odd, w_proj, w_out):
    blocks, rows, cols, chans = x_all.shape
    tiles = blocks * cols // TILE
    width = H * DH
    vmem = pl.BlockSpec(memory_space=pltpu.VMEM)
    smem = pl.BlockSpec(memory_space=pltpu.SMEM)
    anywhere = pl.BlockSpec(memory_space=pl.ANY)
    return pl.pallas_call(
        attention_kernel,
        out_shape=(
            jax.ShapeDtypeStruct((2, rows, TILE, chans), BF16),
            jax.ShapeDtypeStruct((2, rows, TILE, chans), BF16),
            jax.ShapeDtypeStruct((tiles, rows, TILE, chans), BF16),
            jax.ShapeDtypeStruct((2, tiles, TILE, HJ), BF16),
        ),
        in_specs=[smem, smem, anywhere, anywhere, vmem, vmem, vmem, vmem],
        out_specs=(vmem, vmem, anywhere, anywhere),
        scratch_shapes=[
            pltpu.VMEM(x_all.shape, BF16),
            pltpu.VMEM(bias_t.shape, BF16),
            pltpu.VMEM((tiles, rows, TILE, chans), BF16),
            pltpu.VMEM((2, tiles, TILE, HJ), BF16),
            pltpu.SemaphoreType.DMA((blocks,)),
            pltpu.SemaphoreType.DMA((5,)),
            pltpu.VMEM((tiles, rows, TILE, width), BF16),
            pltpu.VMEM((tiles, rows, TILE, width), BF16),
            pltpu.VMEM((2, rows, HJ, width), BF16),
            pltpu.VMEM((2, rows, HJ, width), BF16),
            pltpu.VMEM((CT * TILE, HJ), F32),
            pltpu.VMEM((CT * TILE, HJ), F32),
            pltpu.VMEM((2, rows, 1, HJ), F32),
            pltpu.VMEM((2, rows, 1, HJ), F32),
            pltpu.VMEM((2, rows, 1, HJ), F32),
            pltpu.VMEM((2, rows, width, HJ), F32),
            pltpu.VMEM((2, rows, TILE, width), F32),
            pltpu.VMEM((2, rows, TILE, width), F32),
            pltpu.SMEM((2, tiles + CT), jnp.int32),
            pltpu.VMEM((2, rows, width, HJ), BF16),
            pltpu.VMEM((2, rows, width, HJ), BF16),
        ],
        compiler_params=pltpu.CompilerParams(vmem_limit_bytes=62 * 1024 * 1024),
        name="attention",
    )(place, mask, x_all, bias_t, d_out, d_odd, w_proj, w_out)


MESH = pl.DeviceIdType.MESH
RING = 4


class Links:
    def __init__(self, send_sem, recv_sem):
        self.send_sem, self.recv_sem = send_sem, recv_sem
        self.count = 0
        self.sent = []

    def send(self, src, dst, device):
        n = self.count
        self.count += 1
        copy = pltpu.make_async_remote_copy(
            src_ref=src, dst_ref=dst, send_sem=self.send_sem.at[n], recv_sem=self.recv_sem.at[n],
            device_id=device, device_id_type=MESH,
        )
        copy.start()
        self.sent.append(copy)
        return n

    def arrived(self, n, dst):
        pltpu.make_async_remote_copy(
            src_ref=dst, dst_ref=dst, send_sem=self.send_sem.at[n], recv_sem=self.recv_sem.at[n],
            device_id=self.me, device_id_type=MESH,
        ).wait_recv()

    def finish(self):
        for copy in self.sent:
            copy.wait_send()


class Place:
    def __init__(self):
        self.row = lax.axis_index("row")
        self.col = lax.axis_index("col")
        self.core = self.col % 2
        z = (self.col // 2) % RING
        y = self.col // (2 * RING)
        self.yz = (y, z)

    def col_at(self, steps, core=None):
        y = (self.yz[0] + steps[0]) % RING
        z = (self.yz[1] + steps[1]) % RING
        return y * 2 * RING + z * 2 + (self.core if core is None else core)

    def along(self, axis, step):
        steps = [0, 0]
        steps[axis] = step
        return (self.row, self.col_at(steps))

    def along_x(self, step):
        return ((self.row + step) % RING, self.col)

    def sibling(self):
        return (self.row, self.col_at((0, 0), 1 - self.core))

    def partner(self):
        return (self.row, 8 * RING - 1 - self.col)


def greet(place):
    barrier = pltpu.get_barrier_semaphore()
    others = [place.along(axis, step) for axis in range(2) for step in (1, -1)]
    others += [place.along_x(1), place.along_x(-1), place.sibling(), place.partner()]
    for other in others:
        pl.semaphore_signal(barrier, inc=1, device_id=other, device_id_type=MESH)
    return lambda: pl.semaphore_wait(barrier, len(others))


def normalize(entries):
    centred = entries - jnp.mean(entries, axis=-1, keepdims=True)
    spread = jnp.mean(centred * centred, axis=-1, keepdims=True)
    scale = lax.rsqrt(spread + eps_norm)
    return centred * scale, scale


def pair_steps(axis, first, second):
    return (first, second) if axis == 0 else (second, first)


def gather_kernel(
    slab_ref, bias_in, d_ref, x_all, bias_all, d_odd, x_ref, bias_ref, local_sem, send_sem, recv_sem
):
    place = Place()
    links = Links(send_sem, recv_sem)
    links.me = place.sibling()
    everyone_here = greet(place)
    rows = x_ref.shape[0]
    half = rows // 2

    def turn_bias(a):
        step = 2 * TILE
        for start in range(0, bias_ref.shape[1], step):
            heads = [bias_in[h, a * TILE : (a + 1) * TILE, start : start + step] for h in range(H)]
            bias_ref[a, start : start + step, :] = jnp.transpose(jnp.concatenate(heads, axis=0))

    turn_bias(1)
    everyone_here()
    sub = half // 2
    long = bias_ref.shape[1]
    row = place.row

    def spot(steps, start, size, core=None):
        return x_all.at[place.col_at(steps, core), pl.ds(start, size)]

    def own(start, size):
        return x_ref.at[pl.ds(start, size)]

    def bias_spot(a, step, start=0, size=None):
        return bias_all.at[a, (row + step) % RING, pl.ds(start, long if size is None else size)]

    odd = links.send(bias_ref.at[1], bias_spot(1, 0), place.partner())
    for r in range(rows):
        x_ref[r] = normalize(slab_ref[r].astype(F32))[0].astype(BF16)
    first = {}
    for hf in range(2):
        mine = own(hf * half, half)
        for step in (1, -1):
            first[hf, step] = links.send(mine, spot((0, 0), hf * half, half), place.along(hf, step))
    turn_bias(0)
    bias_direct = {}
    for step in (1, -1):
        bias_direct[0, step] = links.send(bias_ref.at[0], bias_spot(0, 0), place.along_x(step))
    locals_ = [
        pltpu.make_async_copy(x_ref, x_all.at[place.col], local_sem.at[0]),
        pltpu.make_async_copy(bias_ref.at[0], bias_spot(0, 0), local_sem.at[1]),
    ]
    for copy in locals_:
        copy.start()
    second = {}
    chip = {}

    def pass_on(hf, offset, src=None):
        steps = pair_steps(hf, offset, 0)
        there = spot(steps, hf * half, half)
        for step in (1, -1):
            second[hf, offset, step] = links.send(there if src is None else src, there, place.along(1 - hf, step))
        chip[hf, offset, 0] = links.send(there if src is None else src, there, place.sibling())

    links.arrived(odd, bias_spot(1, 0))
    for step in (1, -1):
        bias_direct[1, step] = links.send(bias_spot(1, 0), bias_spot(1, 0), place.along_x(step))
    bias_onward = {}

    def bias_forward(a):
        for step in (1, -1):
            links.arrived(bias_direct[a, step], bias_spot(a, -step))
            piece = bias_spot(a, -step, 0 if step == 1 else long // 2, long // 2)
            bias_onward[a, step] = links.send(piece, piece, place.along_x(step))

    for hf in range(2):
        pass_on(hf, 0, own(hf * half, half))
    d_move = links.send(d_ref.at[:, pl.ds(TILE, TILE)], d_odd, place.partner())

    onward = {}
    for step in (1, -1):
        for hf in range(2):
            links.arrived(first[hf, step], spot(pair_steps(hf, -step, 0), hf * half, half))
            begin = hf * half + (0 if step == 1 else sub)
            piece = spot(pair_steps(hf, -step, 0), begin, sub)
            onward[hf, step] = links.send(piece, piece, place.along(hf, step))
            pass_on(hf, -step)
    for hf in range(2):
        for step in (1, -1):
            begin = hf * half + (0 if step == 1 else sub)
            links.arrived(onward[hf, step], spot(pair_steps(hf, 2, 0), begin, sub))
        pass_on(hf, 2)

    far = {}
    for offset in (0, -1, 1, 2):
        for hf in range(2):
            for step in (1, -1):
                steps = pair_steps(hf, offset, -step)
                links.arrived(second[hf, offset, step], spot(steps, hf * half, half))
                begin = hf * half + (0 if step == 1 else sub)
                piece = spot(steps, begin, sub)
                far[hf, offset, step] = links.send(piece, piece, place.along(1 - hf, step))
                there = spot(steps, hf * half, half)
                chip[hf, offset, step] = links.send(there, there, place.sibling())
        if offset == 0:
            bias_forward(0)
        if offset == 1:
            bias_forward(1)
    for offset in (0, -1, 1, 2):
        for hf in range(2):
            steps = pair_steps(hf, offset, 2)
            for step in (1, -1):
                begin = hf * half + (0 if step == 1 else sub)
                links.arrived(far[hf, offset, step], spot(steps, begin, sub))
            there = spot(steps, hf * half, half)
            chip[hf, offset, 2] = links.send(there, there, place.sibling())
    for a in range(2):
        for step in (1, -1):
            begin = 0 if step == 1 else long // 2
            links.arrived(bias_onward[a, step], bias_spot(a, 2, begin, long // 2))
    links.arrived(d_move, d_odd)
    for (hf, offset, step), n in chip.items():
        steps = pair_steps(hf, offset, -step)
        links.arrived(n, spot(steps, hf * half, half, 1 - place.core))
    links.finish()
    for copy in locals_:
        copy.wait()


def gather(pair_slab, pair_bias, d_out):
    rows, cols, chans = pair_slab.shape
    keys = pair_bias.shape[2]
    anywhere = pl.BlockSpec(memory_space=pl.ANY)
    vmem = pl.BlockSpec(memory_space=pltpu.VMEM)
    copies = 100
    return pl.pallas_call(
        gather_kernel,
        out_shape=(
            jax.ShapeDtypeStruct((8 * RING, rows, cols, chans), BF16),
            jax.ShapeDtypeStruct((2, RING, keys, HJ), BF16),
            jax.ShapeDtypeStruct((rows, TILE, chans), BF16),
        ),
        in_specs=[vmem, vmem, anywhere],
        out_specs=(anywhere,) * 3,
        scratch_shapes=[
            pltpu.VMEM(pair_slab.shape, BF16),
            pltpu.VMEM((2, keys, HJ), BF16),
            pltpu.SemaphoreType.DMA((2,)),
            pltpu.SemaphoreType.DMA((copies,)),
            pltpu.SemaphoreType.DMA((copies,)),
        ],
        compiler_params=pltpu.CompilerParams(
            collective_id=0, has_side_effects=True, vmem_limit_bytes=62 * 1024 * 1024
        ),
        name="gather",
    )(pair_slab, pair_bias, d_out)


def add_into(dst, *sources):
    def step(n, _):
        total = dst[n].astype(F32)
        for source in sources:
            total = total + source[n].astype(F32)
        dst[n] = total.astype(BF16)
        return 0

    lax.fori_loop(0, dst.shape[0], step, 0, unroll=4)


def reduce_kernel(
    pair_ref, grad_ref, out_ref, dn_ref, pair_sum, grad_all, out_odd, dn_odd,
    held, chip_in, one_in, two_in, last_one, last_two, grad_held, grad_one, grad_two,
    local_sem, send_sem, recv_sem, a2a_send, a2a_recv,
):
    place = Place()
    links = Links(send_sem, recv_sem)
    links.me = place.sibling()
    row, col = place.row, place.col
    ncol = grad_all.shape[1]
    rows = pair_ref.shape[2]
    sub = rows // 2
    groups = grad_held.shape[2]

    barrier = pltpu.get_barrier_semaphore()

    def greet_one(d, _):
        pl.semaphore_signal(barrier, inc=1, device_id=(row, (col + d) % ncol), device_id_type=MESH)
        return 0

    lax.fori_loop(1, ncol, greet_one, 0)
    for step in (1, -1):
        pl.semaphore_signal(barrier, inc=1, device_id=place.along_x(step), device_id_type=MESH)
    pl.semaphore_wait(barrier, ncol + 1)

    moves = [links.send(out_ref.at[1], out_odd, place.partner()), links.send(dn_ref.at[1], dn_odd, place.partner())]

    def half_of(step):
        return pl.ds(0 if step == 1 else groups // 2, groups // 2)

    grad_first = {}
    for a in range(2):
        for n, step in enumerate((1, -1)):
            grad_first[a, step] = links.send(
                grad_ref.at[a, (row + 2) % RING, half_of(step)], grad_one.at[a, n], place.along_x(step)
            )
    grad_local = {}
    for a in range(2):
        for rel in (1, 3, 0):
            n = len(grad_local)
            grad_local[a, rel] = pltpu.make_async_copy(
                grad_ref.at[a, (row + rel) % RING], grad_held.at[a, rel], local_sem.at[n]
            )
            grad_local[a, rel].start()

    def slot(hf, i, b):
        dy, dz = pair_steps(hf, i, b)
        return dy, dz, dy * RING + dz

    chip = {}
    local = {}
    for b in (2, 1, 3, 0):
        for hf in range(2):
            for i in (2, 1, 3, 0):
                dy, dz, n = slot(hf, i, b)
                chip[hf, i, b] = links.send(
                    pair_ref.at[place.col_at((dy, dz), 1 - place.core), hf], chip_in.at[n, hf], place.sibling()
                )
                local[hf, i, b] = pltpu.make_async_copy(
                    pair_ref.at[place.col_at((dy, dz)), hf], held.at[n, hf], local_sem.at[6 + len(local)]
                )
                local[hf, i, b].start()

    def collect(hf, i, b):
        n = slot(hf, i, b)[2]
        local[hf, i, b].wait()
        links.arrived(chip[hf, i, b], chip_in.at[n, hf])
        add_into(held.at[n, hf], chip_in.at[n, hf])
        return held.at[n, hf]

    def sub_of(step):
        return pl.ds(0 if step == 1 else sub, sub)

    one = {}
    for hf in range(2):
        for i in (2, 1, 3, 0):
            block = collect(hf, i, 2)
            for n, step in enumerate((1, -1)):
                one[hf, i, step] = links.send(
                    block.at[sub_of(step)], one_in.at[hf, i, n], place.along(1 - hf, step)
                )

    grad_second = {}
    for a in range(2):
        for n, step in enumerate((1, -1)):
            rel = step % RING
            grad_local[a, rel].wait()
            links.arrived(grad_first[a, step], grad_one.at[a, n])
            add_into(grad_held.at[a, rel, half_of(step)], grad_one.at[a, n])
            grad_second[a, step] = links.send(grad_held.at[a, rel], grad_two.at[a, n], place.along_x(step))

    two = {}
    for n, step in enumerate((1, -1)):
        for hf in range(2):
            for i in (2, 1, 3, 0):
                block = collect(hf, i, step % RING)
                links.arrived(one[hf, i, step], one_in.at[hf, i, n])
                add_into(block.at[sub_of(step)], one_in.at[hf, i, n])
                two[hf, i, step] = links.send(block, two_in.at[hf, i, n], place.along(1 - hf, step))
    mine = {(hf, i): collect(hf, i, 0) for hf in range(2) for i in (2, 1, 3, 0)}

    per = grad_all.shape[2]

    def keys_of(a, device):
        return grad_held.at[a, 0, pl.ds(device * per, per)]

    def a2a(a, d):
        target = (col + d) % ncol
        return pltpu.make_async_remote_copy(
            src_ref=keys_of(a, target), dst_ref=grad_all.at[a, col],
            send_sem=a2a_send.at[a, d], recv_sem=a2a_recv.at[a, d],
            device_id=(row, target), device_id_type=MESH,
        )

    def a2a_back(a, d):
        source = (col - d) % ncol
        return pltpu.make_async_remote_copy(
            src_ref=keys_of(a, source), dst_ref=grad_all.at[a, source],
            send_sem=a2a_send.at[a, d], recv_sem=a2a_recv.at[a, d],
            device_id=(row, source), device_id_type=MESH,
        )

    keep = []

    def finish_bias(a):
        grad_local[a, 0].wait()
        for n, step in enumerate((1, -1)):
            links.arrived(grad_second[a, step], grad_two.at[a, n])
        add_into(grad_held.at[a, 0], grad_two.at[a, 0], grad_two.at[a, 1])

        def start(d, _):
            a2a(a, d).start()
            return 0

        lax.fori_loop(1, ncol, start, 0)
        keep.append(pltpu.make_async_copy(keys_of(a, col), grad_all.at[a, col], local_sem.at[38 + a]))
        keep[-1].start()

    finish_bias(0)

    tail_one, tail_two = {}, {}
    for i in (2, 1, 3, 0):
        for hf in range(2):
            block = mine[hf, i]
            for n, step in enumerate((1, -1)):
                links.arrived(two[hf, i, step], two_in.at[hf, i, n])
            add_into(block, two_in.at[hf, i, 0], two_in.at[hf, i, 1])
            if i == 2:
                for n, step in enumerate((1, -1)):
                    tail_one[hf, step] = links.send(
                        block.at[sub_of(step)], last_one.at[hf, n], place.along(hf, step)
                    )
            elif i != 0:
                n, step = (0, 1) if i == 1 else (1, -1)
                links.arrived(tail_one[hf, step], last_one.at[hf, n])
                add_into(block.at[sub_of(step)], last_one.at[hf, n])
                tail_two[hf, step] = links.send(block, last_two.at[hf, n], place.along(hf, step))
    finish_bias(1)

    for hf in range(2):
        block = mine[hf, 0]
        for n, step in enumerate((1, -1)):
            links.arrived(tail_two[hf, step], last_two.at[hf, n])
        add_into(block, last_two.at[hf, 0], last_two.at[hf, 1])
        pair_sum[hf] = block[...]

    def a2a_end(d, _):
        for a in range(2):
            a2a_back(a, d).wait_recv()
            a2a(a, d).wait_send()
        return 0

    lax.fori_loop(1, ncol, a2a_end, 0)
    links.arrived(moves[0], out_odd)
    links.arrived(moves[1], dn_odd)
    links.finish()
    for copy in keep:
        copy.wait()


def reduce(pair, bias_grad, out, dn):
    ncol = 8 * RING
    rows, cols, chans = out.shape[1:]
    pair = pair.reshape(ncol, 2, rows, cols, chans)
    keys = bias_grad.shape[1] * TILE // RING
    unit = 32
    grads = bias_grad.reshape(2, RING, keys // unit, unit, HJ)
    part = keys // ncol
    anywhere = pl.BlockSpec(memory_space=pl.ANY)
    vmem = pl.BlockSpec(memory_space=pltpu.VMEM)
    block = (rows, cols, chans)
    half = (rows // 2, cols, chans)
    return pl.pallas_call(
        reduce_kernel,
        out_shape=(
            jax.ShapeDtypeStruct((2,) + block, BF16),
            jax.ShapeDtypeStruct((2, ncol, part // unit, unit, HJ), BF16),
            jax.ShapeDtypeStruct(block, BF16),
            jax.ShapeDtypeStruct(block, BF16),
        ),
        in_specs=[anywhere] * 4,
        out_specs=(vmem, anywhere, anywhere, anywhere),
        scratch_shapes=[
            pltpu.VMEM((RING * RING, 2) + block, BF16),
            pltpu.VMEM((RING * RING, 2) + block, BF16),
            pltpu.VMEM((2, RING, 2) + half, BF16),
            pltpu.VMEM((2, RING, 2) + block, BF16),
            pltpu.VMEM((2, 2) + half, BF16),
            pltpu.VMEM((2, 2) + block, BF16),
            pltpu.VMEM((2, RING, keys // unit, unit, HJ), BF16),
            pltpu.VMEM((2, 2, keys // unit // 2, unit, HJ), BF16),
            pltpu.VMEM((2, 2, keys // unit, unit, HJ), BF16),
            pltpu.SemaphoreType.DMA((40,)),
            pltpu.SemaphoreType.DMA((90,)),
            pltpu.SemaphoreType.DMA((90,)),
            pltpu.SemaphoreType.DMA((2, ncol)),
            pltpu.SemaphoreType.DMA((2, ncol)),
        ],
        compiler_params=pltpu.CompilerParams(
            collective_id=1, has_side_effects=True, vmem_limit_bytes=62 * 1024 * 1024
        ),
        name="reduce",
    )(pair, grads, out, dn)


def finish_kernel(
    slab_ref, out_ref, out_odd_ref, dn_ref, dn_odd_ref, pair_ref, grad_ref,
    attn_ref, slab_grad_ref, bias_grad_ref,
):
    count = grad_ref.shape[1]
    rows = slab_ref.shape[0]
    for m in range(count):
        even = grad_ref[0, m].astype(F32)
        odd = grad_ref[1, count - 1 - m].astype(F32)
        for h in range(H):
            part = slice(h * TILE, (h + 1) * TILE)
            both = jnp.concatenate([even[:, part], odd[:, part]], axis=1)
            bias_grad_ref[:, h, 2 * TILE * m : 2 * TILE * (m + 1)] = both
    for r in range(rows):
        for a in range(2):
            part = slice(a * TILE, (a + 1) * TILE)
            attn_ref[r, part] = out_ref[0, r] if a == 0 else out_odd_ref[r]
            d_own = dn_ref[0, r] if a == 0 else dn_odd_ref[r]
            d_normed = d_own.astype(F32) + pair_ref[a, r].astype(F32)
            normed, scale = normalize(slab_ref[r, part].astype(F32))
            d_mean = jnp.mean(d_normed, axis=-1, keepdims=True)
            d_along = jnp.mean(d_normed * normed, axis=-1, keepdims=True)
            slab_grad_ref[r, part] = (scale * (d_normed - d_mean - normed * d_along)).astype(BF16)


def finish(pair_slab, out, out_odd, dn, dn_odd, pair_sum, grads):
    count, keys = grads.shape[1:3]
    vmem = pl.BlockSpec(memory_space=pltpu.VMEM)
    return pl.pallas_call(
        finish_kernel,
        out_shape=(
            jax.ShapeDtypeStruct(pair_slab.shape, BF16),
            jax.ShapeDtypeStruct(pair_slab.shape, BF16),
            jax.ShapeDtypeStruct((keys, H, 2 * TILE * count), F32),
        ),
        in_specs=[vmem] * 7,
        out_specs=(vmem,) * 3,
        compiler_params=pltpu.CompilerParams(vmem_limit_bytes=62 * 1024 * 1024),
        name="finish",
    )(pair_slab, out, out_odd, dn, dn_odd, pair_sum, grads)


def on_device(pair_slab, pair_bias, tile_mask, w_proj, w_out, d_out):
    ncol = lax.axis_size("col")
    c = lax.axis_index("col")
    x_all, bias_all, d_odd = gather(pair_slab, pair_bias, d_out)
    bias_t = bias_all.reshape(2, -1, TILE, HJ)
    out, dn, pair, bias_grad = attention(
        c.reshape(1).astype(jnp.int32), tile_mask, x_all, bias_t, d_out, d_odd, w_proj, w_out
    )
    pair_sum, grads, out_odd, dn_odd = reduce(pair, bias_grad, out, dn)
    return finish(pair_slab, out, out_odd, dn, dn_odd, pair_sum, grads.reshape(2, ncol, -1, HJ))


def solution(mesh):
    in_specs = (P("row", "col", None), P(None, "col", "row"), P(), P(), P(), P("row", "col", None))
    out_specs = (P("row", "col", None), P("row", "col", None), P(("row", "col"), None, None))
    return jax.shard_map(
        on_device, mesh=mesh, in_specs=in_specs, out_specs=out_specs, check_vma=False
    )
```

```python
import functools

import jax
import jax.numpy as jnp
from jax import lax
from jax.experimental import pallas as pl
from jax.experimental.pallas import tpu as pltpu
from jax.sharding import PartitionSpec as P

H = 4
DH = 32
TILE = 64
HJ = H * TILE

eps_norm = 1e-05
neg_big = -1e30
CT = 8
GROUP = 8
SKEW = 2
F32 = jnp.float32
BF16 = jnp.bfloat16


def nt(a, b):
    return lax.dot_general(a, b, (((1,), (1,)), ((), ())), preferred_element_type=F32)


def tn(a, b):
    return lax.dot_general(a, b, (((0,), (0,)), ((), ())), preferred_element_type=F32)


def nn(a, b):
    return jnp.dot(a, b, preferred_element_type=F32)


def head_blocks(rows, chans):
    row_head = lax.broadcasted_iota(jnp.int32, (rows, chans), 0) // TILE
    col_head = lax.broadcasted_iota(jnp.int32, (rows, chans), 1) // DH
    return row_head == col_head


def diagonal(full_t):
    parts = [full_t[h * DH : (h + 1) * DH, h * TILE : (h + 1) * TILE] for h in range(H)]
    return jnp.transpose(jnp.concatenate(parts, axis=0))


def attention_kernel(
    place_ref, mask_ref, x_far, bias_far, d_out_ref, d_odd_ref, w_proj_ref, w_out_ref,
    out_ref, dn_ref, pair_far, bias_grad_far,
    x_ref, bias_ref, pair_ref, bias_grad_ref, x_sem, move_sem,
    k_ref, v_ref, q_ref, do_ref, bias_f, grad_f, max_ref, sum_ref, delta_ref, acc_ref,
    gate_ref, dg_ref, list_ref, qt_ref, dt_ref,
):
    c = place_ref[0]
    tiles = 2 * x_ref.shape[0]
    used = jnp.maximum(c, tiles // 2 - 1 - c) + 1

    def fetch(block):
        return pltpu.make_async_copy(x_far.at[block], x_ref.at[block], x_sem.at[block])

    def fetch_start(block, _):
        fetch(block).start()
        return 0

    lax.fori_loop(0, used, fetch_start, 0)
    bias_moves = [
        pltpu.make_async_copy(bias_far.at[a], bias_ref.at[a], move_sem.at[a]) for a in range(2)
    ]
    grad_moves = [
        pltpu.make_async_copy(bias_grad_ref.at[a], bias_grad_far.at[a], move_sem.at[2 + a]) for a in range(2)
    ]
    pair_move = pltpu.make_async_copy(pair_ref, pair_far, move_sem.at[4])
    for move in bias_moves:
        move.start()
    rows = x_ref.shape[1]
    width = H * DH
    q_scale = DH ** (-0.5)
    query_tiles = (2 * c, tiles - 1 - 2 * c)
    w_q = w_proj_ref[:, :width]
    w_pair = w_proj_ref[:, width : 3 * width]
    w_gate = w_proj_ref[:, 3 * width :]
    w_pair_t = jnp.transpose(w_pair)

    def clear(b, _):
        pair_ref[b] = jnp.zeros(pair_ref.shape[1:], BF16)
        for a in range(2):
            bias_grad_ref[a, b] = jnp.zeros(bias_grad_ref.shape[2:], BF16)
        return 0

    lax.fori_loop(0, tiles, clear, 0)

    def project(block, _):
        fetch(block).wait()
        kv = nn(x_ref[block].reshape(rows * 2 * TILE, -1), w_pair).astype(BF16)
        kv = kv.reshape(rows, 2 * TILE, 2 * width)
        for half in range(2):
            k_ref[2 * block + half] = kv[:, half * TILE : (half + 1) * TILE, :width]
            v_ref[2 * block + half] = kv[:, half * TILE : (half + 1) * TILE, width:]
        return 0

    lax.fori_loop(0, used, project, 0)

    counts, idles = [], []
    for a in range(2):
        def scan_tile(b, carried, a=a):
            count, idle = carried
            live = mask_ref[query_tiles[a], b] > 0
            list_ref[a, count] = b
            return jnp.where(live, count + 1, count), jnp.where(live, idle, b)

        count, idle = lax.fori_loop(0, tiles, scan_tile, (jnp.int32(0), jnp.int32(0)))
        for extra in range(CT):
            list_ref[a, count + extra] = query_tiles[a]
        counts.append(count)
        idles.append(idle)

    blocks = head_blocks(HJ, width)
    zero = jnp.zeros((HJ, width), BF16)
    for a in range(2):
        tile = query_tiles[a]
        x_q = x_ref[tile // 2, :, pl.ds(pl.multiple_of((tile % 2) * TILE, TILE), TILE), :]
        x_q = x_q.reshape(rows * TILE, -1)
        queries = (nn(x_q, w_q) * q_scale).astype(BF16)
        gating = jax.nn.sigmoid(nn(x_q, w_gate))
        d_out = d_out_ref[:, :TILE] if a == 0 else d_odd_ref[...]
        d_gated = nt(d_out.reshape(rows * TILE, -1), w_out_ref[...])
        d_att = (d_gated * gating).astype(BF16)
        gate_ref[a] = gating.reshape(rows, TILE, width)
        dg_ref[a] = d_gated.reshape(rows, TILE, width)
        for r in range(rows):
            part = slice(r * TILE, (r + 1) * TILE)
            q = jnp.where(blocks, jnp.concatenate([queries[part]] * H, axis=0), zero)
            do = jnp.where(blocks, jnp.concatenate([d_att[part]] * H, axis=0), zero)
            q_ref[a, r] = q
            do_ref[a, r] = do
            qt_ref[a, r] = jnp.transpose(q)
            dt_ref[a, r] = jnp.transpose(do)

    def load_chunk(a, start, ct):
        ids = [list_ref[a, start + t] for t in range(ct)]
        for t in range(ct):
            block = bias_ref[a, ids[t]].astype(F32)
            shut = jnp.where(start + t < counts[a], 0.0, neg_big)
            bias_f[t * TILE : (t + 1) * TILE, :] = block + shut
        return ids

    def walk(a, chunk):
        full = (counts[a] + CT // 2 - 1) // CT

        def step(n, _):
            chunk(a, n * CT, CT)
            return 0

        lax.fori_loop(0, full, step, 0)

        @pl.when(counts[a] > full * CT)
        def _():
            chunk(a, full * CT, CT // 2)

    max_ref[...] = jnp.full(max_ref.shape, neg_big, F32)
    sum_ref[...] = jnp.zeros(sum_ref.shape, F32)
    acc_ref[...] = jnp.zeros(acc_ref.shape, F32)
    def forward(a, start, ct):
        ids = load_chunk(a, start, ct)

        def score(r):
            keys = jnp.concatenate([k_ref[i, r] for i in ids], axis=0)
            return nn(keys, qt_ref[a, r]) + bias_f[: ct * TILE, :]

        def use(r, scores):
            values = jnp.concatenate([v_ref[i, r] for i in ids], axis=0)
            old = max_ref[a, r]
            new = jnp.maximum(old, jnp.max(scores, axis=0, keepdims=True))
            fade = jnp.exp(old - new)
            probs = jnp.exp(scores - new)
            max_ref[a, r] = new
            sum_ref[a, r] = sum_ref[a, r] * fade + jnp.sum(probs, axis=0, keepdims=True)
            acc_ref[a, r] = acc_ref[a, r] * fade + tn(values, probs.astype(BF16))

        def some_rows(step, _):
            waiting = []
            for u in range(GROUP + SKEW):
                if u < GROUP:
                    waiting.append(score(step * GROUP + u))
                if u >= SKEW:
                    use(step * GROUP + u - SKEW, waiting.pop(0))
            return 0

        lax.fori_loop(0, rows // GROUP, some_rows, 0)

    for a in range(2):
        bias_moves[a].wait()
        walk(a, forward)

    for a in range(2):
        attended = []
        for r in range(rows):
            total = sum_ref[a, r]
            full_t = acc_ref[a, r] * (1.0 / total)
            max_ref[a, r] = max_ref[a, r] + jnp.log(total)
            delta_ref[a, r] = jnp.sum(full_t * dt_ref[a, r].astype(F32), axis=0, keepdims=True)
            attended.append(diagonal(full_t))
            acc_ref[a, r] = jnp.zeros(acc_ref.shape[2:], F32)
        attended = jnp.concatenate(attended, axis=0).reshape(rows, TILE, width)
        gating = gate_ref[a]
        gated = (gating * attended).astype(BF16).reshape(rows * TILE, width)
        out_ref[a] = nn(gated, w_out_ref[...]).astype(BF16).reshape(rows, TILE, -1)
        dg_ref[a] = dg_ref[a] * attended * gating * (1.0 - gating)

    def backward(a, start, ct):
        ids = load_chunk(a, start, ct)

        def score(r):
            keys = jnp.concatenate([k_ref[i, r] for i in ids], axis=0)
            values = jnp.concatenate([v_ref[i, r] for i in ids], axis=0)
            return nn(keys, qt_ref[a, r]) + bias_f[: ct * TILE, :], nn(values, dt_ref[a, r])

        def use(r, made, first):
            scores, d_probs = made
            keys = jnp.concatenate([k_ref[i, r] for i in ids], axis=0)
            probs = jnp.exp(scores - max_ref[a, r])
            d_scores = probs * (d_probs - delta_ref[a, r])
            if first is None:
                grad_f[: ct * TILE, :] += d_scores
            else:
                grad_f[: ct * TILE, :] = jnp.where(first, d_scores, grad_f[: ct * TILE, :] + d_scores)
            d_b = d_scores.astype(BF16)
            acc_ref[a, r] += tn(keys, d_b)
            d_keys = nn(d_b, q_ref[a, r])
            d_values = nn(probs.astype(BF16), do_ref[a, r])
            both = jnp.concatenate([d_keys, d_values], axis=1).astype(BF16)
            term = nn(both, w_pair_t)
            for t in range(ct):
                piece = term[t * TILE : (t + 1) * TILE]
                pair_ref[ids[t], r] = (pair_ref[ids[t], r].astype(F32) + piece).astype(BF16)

        def some_rows(step, _):
            waiting = []
            for u in range(GROUP + SKEW):
                if u < GROUP:
                    waiting.append(score(step * GROUP + u))
                if u >= SKEW:
                    first = (step == 0) if u == SKEW else None
                    use(step * GROUP + u - SKEW, waiting.pop(0), first)
            return 0

        lax.fori_loop(0, rows // GROUP, some_rows, 0)
        for t in range(ct):
            target = jnp.where(start + t < counts[a], ids[t], idles[a])
            bias_grad_ref[a, target] = grad_f[t * TILE : (t + 1) * TILE, :].astype(BF16)

    for a in range(2):
        walk(a, backward)
        grad_moves[a].start()
    pair_move.start()

    for a in range(2):
        d_q = jnp.concatenate([diagonal(acc_ref[a, r]) for r in range(rows)], axis=0) * q_scale
        d_gate = dg_ref[a].reshape(rows * TILE, width)
        total = nt(d_q.astype(BF16), w_q) + nt(d_gate.astype(BF16), w_gate)
        dn_ref[a] = total.astype(BF16).reshape(rows, TILE, -1)
    for move in grad_moves + [pair_move]:
        move.wait()


def attention(place, mask, x_all, bias_t, d_out, d_odd, w_proj, w_out):
    blocks, rows, cols, chans = x_all.shape
    tiles = blocks * cols // TILE
    width = H * DH
    vmem = pl.BlockSpec(memory_space=pltpu.VMEM)
    smem = pl.BlockSpec(memory_space=pltpu.SMEM)
    anywhere = pl.BlockSpec(memory_space=pl.ANY)
    return pl.pallas_call(
        attention_kernel,
        out_shape=(
            jax.ShapeDtypeStruct((2, rows, TILE, chans), BF16),
            jax.ShapeDtypeStruct((2, rows, TILE, chans), BF16),
            jax.ShapeDtypeStruct((tiles, rows, TILE, chans), BF16),
            jax.ShapeDtypeStruct((2, tiles, TILE, HJ), BF16),
        ),
        in_specs=[smem, smem, anywhere, anywhere, vmem, vmem, vmem, vmem],
        out_specs=(vmem, vmem, anywhere, anywhere),
        scratch_shapes=[
            pltpu.VMEM(x_all.shape, BF16),
            pltpu.VMEM(bias_t.shape, BF16),
            pltpu.VMEM((tiles, rows, TILE, chans), BF16),
            pltpu.VMEM((2, tiles, TILE, HJ), BF16),
            pltpu.SemaphoreType.DMA((blocks,)),
            pltpu.SemaphoreType.DMA((5,)),
            pltpu.VMEM((tiles, rows, TILE, width), BF16),
            pltpu.VMEM((tiles, rows, TILE, width), BF16),
            pltpu.VMEM((2, rows, HJ, width), BF16),
            pltpu.VMEM((2, rows, HJ, width), BF16),
            pltpu.VMEM((CT * TILE, HJ), F32),
            pltpu.VMEM((CT * TILE, HJ), F32),
            pltpu.VMEM((2, rows, 1, HJ), F32),
            pltpu.VMEM((2, rows, 1, HJ), F32),
            pltpu.VMEM((2, rows, 1, HJ), F32),
            pltpu.VMEM((2, rows, width, HJ), F32),
            pltpu.VMEM((2, rows, TILE, width), F32),
            pltpu.VMEM((2, rows, TILE, width), F32),
            pltpu.SMEM((2, tiles + CT), jnp.int32),
            pltpu.VMEM((2, rows, width, HJ), BF16),
            pltpu.VMEM((2, rows, width, HJ), BF16),
        ],
        compiler_params=pltpu.CompilerParams(vmem_limit_bytes=62 * 1024 * 1024),
        name="attention",
    )(place, mask, x_all, bias_t, d_out, d_odd, w_proj, w_out)


MESH = pl.DeviceIdType.MESH
RING = 4


class Links:
    def __init__(self, send_sem, recv_sem):
        self.send_sem, self.recv_sem = send_sem, recv_sem
        self.count = 0
        self.sent = []

    def send(self, src, dst, device):
        n = self.count
        self.count += 1
        copy = pltpu.make_async_remote_copy(
            src_ref=src, dst_ref=dst, send_sem=self.send_sem.at[n], recv_sem=self.recv_sem.at[n],
            device_id=device, device_id_type=MESH,
        )
        copy.start()
        self.sent.append(copy)
        return n

    def arrived(self, n, dst):
        pltpu.make_async_remote_copy(
            src_ref=dst, dst_ref=dst, send_sem=self.send_sem.at[n], recv_sem=self.recv_sem.at[n],
            device_id=self.me, device_id_type=MESH,
        ).wait_recv()

    def finish(self):
        for copy in self.sent:
            copy.wait_send()


class Place:
    def __init__(self):
        self.row = lax.axis_index("row")
        self.col = lax.axis_index("col")
        self.core = self.col % 2
        z = (self.col // 2) % RING
        y = self.col // (2 * RING)
        self.yz = (y, z)

    def col_at(self, steps, core=None):
        y = (self.yz[0] + steps[0]) % RING
        z = (self.yz[1] + steps[1]) % RING
        return y * 2 * RING + z * 2 + (self.core if core is None else core)

    def along(self, axis, step):
        steps = [0, 0]
        steps[axis] = step
        return (self.row, self.col_at(steps))

    def along_x(self, step):
        return ((self.row + step) % RING, self.col)

    def sibling(self):
        return (self.row, self.col_at((0, 0), 1 - self.core))

    def partner(self):
        return (self.row, 8 * RING - 1 - self.col)


def greet(place):
    barrier = pltpu.get_barrier_semaphore()
    others = [place.along(axis, step) for axis in range(2) for step in (1, -1)]
    others += [place.along_x(1), place.along_x(-1), place.sibling(), place.partner()]
    for other in others:
        pl.semaphore_signal(barrier, inc=1, device_id=other, device_id_type=MESH)
    return lambda: pl.semaphore_wait(barrier, len(others))


def normalize(entries):
    centred = entries - jnp.mean(entries, axis=-1, keepdims=True)
    spread = jnp.mean(centred * centred, axis=-1, keepdims=True)
    scale = lax.rsqrt(spread + eps_norm)
    return centred * scale, scale


def pair_steps(axis, first, second):
    return (first, second) if axis == 0 else (second, first)


def gather_kernel(
    slab_ref, bias_in, d_ref, x_all, bias_all, d_odd, x_ref, bias_ref, local_sem, send_sem, recv_sem
):
    place = Place()
    links = Links(send_sem, recv_sem)
    links.me = place.sibling()
    everyone_here = greet(place)
    rows = x_ref.shape[0]
    half = rows // 2

    def turn_bias(a):
        step = 2 * TILE
        for start in range(0, bias_ref.shape[1], step):
            heads = [bias_in[h, a * TILE : (a + 1) * TILE, start : start + step] for h in range(H)]
            bias_ref[a, start : start + step, :] = jnp.transpose(jnp.concatenate(heads, axis=0))

    turn_bias(1)
    everyone_here()
    sub = half // 2
    long = bias_ref.shape[1]
    row = place.row

    def spot(steps, start, size, core=None):
        return x_all.at[place.col_at(steps, core), pl.ds(start, size)]

    def own(start, size):
        return x_ref.at[pl.ds(start, size)]

    def bias_spot(a, step, start=0, size=None):
        return bias_all.at[a, (row + step) % RING, pl.ds(start, long if size is None else size)]

    odd = links.send(bias_ref.at[1], bias_spot(1, 0), place.partner())
    for r in range(rows):
        x_ref[r] = normalize(slab_ref[r].astype(F32))[0].astype(BF16)
    first = {}
    for hf in range(2):
        mine = own(hf * half, half)
        for step in (1, -1):
            first[hf, step] = links.send(mine, spot((0, 0), hf * half, half), place.along(hf, step))
    turn_bias(0)
    bias_direct = {}
    for step in (1, -1):
        bias_direct[0, step] = links.send(bias_ref.at[0], bias_spot(0, 0), place.along_x(step))
    locals_ = [
        pltpu.make_async_copy(x_ref, x_all.at[place.col], local_sem.at[0]),
        pltpu.make_async_copy(bias_ref.at[0], bias_spot(0, 0), local_sem.at[1]),
    ]
    for copy in locals_:
        copy.start()
    second = {}
    chip = {}

    def pass_on(hf, offset, src=None):
        steps = pair_steps(hf, offset, 0)
        there = spot(steps, hf * half, half)
        for step in (1, -1):
            second[hf, offset, step] = links.send(there if src is None else src, there, place.along(1 - hf, step))
        chip[hf, offset, 0] = links.send(there if src is None else src, there, place.sibling())

    links.arrived(odd, bias_spot(1, 0))
    for step in (1, -1):
        bias_direct[1, step] = links.send(bias_spot(1, 0), bias_spot(1, 0), place.along_x(step))
    bias_onward = {}

    def bias_forward(a):
        for step in (1, -1):
            links.arrived(bias_direct[a, step], bias_spot(a, -step))
            piece = bias_spot(a, -step, 0 if step == 1 else long // 2, long // 2)
            bias_onward[a, step] = links.send(piece, piece, place.along_x(step))

    for hf in range(2):
        pass_on(hf, 0, own(hf * half, half))
    d_move = links.send(d_ref.at[:, pl.ds(TILE, TILE)], d_odd, place.partner())

    onward = {}
    for step in (1, -1):
        for hf in range(2):
            links.arrived(first[hf, step], spot(pair_steps(hf, -step, 0), hf * half, half))
            begin = hf * half + (0 if step == 1 else sub)
            piece = spot(pair_steps(hf, -step, 0), begin, sub)
            onward[hf, step] = links.send(piece, piece, place.along(hf, step))
            pass_on(hf, -step)
    for hf in range(2):
        for step in (1, -1):
            begin = hf * half + (0 if step == 1 else sub)
            links.arrived(onward[hf, step], spot(pair_steps(hf, 2, 0), begin, sub))
        pass_on(hf, 2)

    far = {}
    for offset in (0, -1, 1, 2):
        for hf in range(2):
            for step in (1, -1):
                steps = pair_steps(hf, offset, -step)
                links.arrived(second[hf, offset, step], spot(steps, hf * half, half))
                begin = hf * half + (0 if step == 1 else sub)
                piece = spot(steps, begin, sub)
                far[hf, offset, step] = links.send(piece, piece, place.along(1 - hf, step))
                there = spot(steps, hf * half, half)
                chip[hf, offset, step] = links.send(there, there, place.sibling())
        if offset == 0:
            bias_forward(0)
        if offset == 1:
            bias_forward(1)
    for offset in (0, -1, 1, 2):
        for hf in range(2):
            steps = pair_steps(hf, offset, 2)
            for step in (1, -1):
                begin = hf * half + (0 if step == 1 else sub)
                links.arrived(far[hf, offset, step], spot(steps, begin, sub))
            there = spot(steps, hf * half, half)
            chip[hf, offset, 2] = links.send(there, there, place.sibling())
    for a in range(2):
        for step in (1, -1):
            begin = 0 if step == 1 else long // 2
            links.arrived(bias_onward[a, step], bias_spot(a, 2, begin, long // 2))
    links.arrived(d_move, d_odd)
    for (hf, offset, step), n in chip.items():
        steps = pair_steps(hf, offset, -step)
        links.arrived(n, spot(steps, hf * half, half, 1 - place.core))
    links.finish()
    for copy in locals_:
        copy.wait()


def gather(pair_slab, pair_bias, d_out):
    rows, cols, chans = pair_slab.shape
    keys = pair_bias.shape[2]
    anywhere = pl.BlockSpec(memory_space=pl.ANY)
    vmem = pl.BlockSpec(memory_space=pltpu.VMEM)
    copies = 100
    return pl.pallas_call(
        gather_kernel,
        out_shape=(
            jax.ShapeDtypeStruct((8 * RING, rows, cols, chans), BF16),
            jax.ShapeDtypeStruct((2, RING, keys, HJ), BF16),
            jax.ShapeDtypeStruct((rows, TILE, chans), BF16),
        ),
        in_specs=[vmem, vmem, anywhere],
        out_specs=(anywhere,) * 3,
        scratch_shapes=[
            pltpu.VMEM(pair_slab.shape, BF16),
            pltpu.VMEM((2, keys, HJ), BF16),
            pltpu.SemaphoreType.DMA((2,)),
            pltpu.SemaphoreType.DMA((copies,)),
            pltpu.SemaphoreType.DMA((copies,)),
        ],
        compiler_params=pltpu.CompilerParams(
            collective_id=0, has_side_effects=True, vmem_limit_bytes=62 * 1024 * 1024
        ),
        name="gather",
    )(pair_slab, pair_bias, d_out)


def add_into(dst, *sources):
    def step(n, _):
        total = dst[n].astype(F32)
        for source in sources:
            total = total + source[n].astype(F32)
        dst[n] = total.astype(BF16)
        return 0

    lax.fori_loop(0, dst.shape[0], step, 0, unroll=4)


def reduce_kernel(
    pair_ref, grad_ref, out_ref, dn_ref, pair_sum, grad_all, out_odd, dn_odd,
    held, chip_in, one_in, two_in, last_one, last_two, grad_held, grad_one, grad_two,
    local_sem, send_sem, recv_sem, a2a_send, a2a_recv,
):
    place = Place()
    links = Links(send_sem, recv_sem)
    links.me = place.sibling()
    row, col = place.row, place.col
    ncol = grad_all.shape[1]
    rows = pair_ref.shape[2]
    sub = rows // 2
    groups = grad_held.shape[2]

    barrier = pltpu.get_barrier_semaphore()

    def greet_one(d, _):
        pl.semaphore_signal(barrier, inc=1, device_id=(row, (col + d) % ncol), device_id_type=MESH)
        return 0

    lax.fori_loop(1, ncol, greet_one, 0)
    for step in (1, -1):
        pl.semaphore_signal(barrier, inc=1, device_id=place.along_x(step), device_id_type=MESH)
    pl.semaphore_wait(barrier, ncol + 1)

    moves = [links.send(out_ref.at[1], out_odd, place.partner()), links.send(dn_ref.at[1], dn_odd, place.partner())]

    def half_of(step):
        return pl.ds(0 if step == 1 else groups // 2, groups // 2)

    grad_first = {}
    for a in range(2):
        for n, step in enumerate((1, -1)):
            grad_first[a, step] = links.send(
                grad_ref.at[a, (row + 2) % RING, half_of(step)], grad_one.at[a, n], place.along_x(step)
            )
    grad_local = {}
    for a in range(2):
        for rel in (1, 3, 0):
            n = len(grad_local)
            grad_local[a, rel] = pltpu.make_async_copy(
                grad_ref.at[a, (row + rel) % RING], grad_held.at[a, rel], local_sem.at[n]
            )
            grad_local[a, rel].start()

    def slot(hf, i, b):
        dy, dz = pair_steps(hf, i, b)
        return dy, dz, dy * RING + dz

    chip = {}
    local = {}
    for b in (2, 1, 3, 0):
        for hf in range(2):
            for i in (2, 1, 3, 0):
                dy, dz, n = slot(hf, i, b)
                chip[hf, i, b] = links.send(
                    pair_ref.at[place.col_at((dy, dz), 1 - place.core), hf], chip_in.at[n, hf], place.sibling()
                )
                local[hf, i, b] = pltpu.make_async_copy(
                    pair_ref.at[place.col_at((dy, dz)), hf], held.at[n, hf], local_sem.at[6 + len(local)]
                )
                local[hf, i, b].start()

    def collect(hf, i, b):
        n = slot(hf, i, b)[2]
        local[hf, i, b].wait()
        links.arrived(chip[hf, i, b], chip_in.at[n, hf])
        add_into(held.at[n, hf], chip_in.at[n, hf])
        return held.at[n, hf]

    def sub_of(step):
        return pl.ds(0 if step == 1 else sub, sub)

    one = {}
    for hf in range(2):
        for i in (2, 1, 3, 0):
            block = collect(hf, i, 2)
            for n, step in enumerate((1, -1)):
                one[hf, i, step] = links.send(
                    block.at[sub_of(step)], one_in.at[hf, i, n], place.along(1 - hf, step)
                )

    grad_second = {}
    for a in range(2):
        for n, step in enumerate((1, -1)):
            rel = step % RING
            grad_local[a, rel].wait()
            links.arrived(grad_first[a, step], grad_one.at[a, n])
            add_into(grad_held.at[a, rel, half_of(step)], grad_one.at[a, n])
            grad_second[a, step] = links.send(grad_held.at[a, rel], grad_two.at[a, n], place.along_x(step))

    two = {}
    for n, step in enumerate((1, -1)):
        for hf in range(2):
            for i in (2, 1, 3, 0):
                block = collect(hf, i, step % RING)
                links.arrived(one[hf, i, step], one_in.at[hf, i, n])
                add_into(block.at[sub_of(step)], one_in.at[hf, i, n])
                two[hf, i, step] = links.send(block, two_in.at[hf, i, n], place.along(1 - hf, step))
    mine = {(hf, i): collect(hf, i, 0) for hf in range(2) for i in (2, 1, 3, 0)}

    per = grad_all.shape[2]

    def keys_of(a, device):
        return grad_held.at[a, 0, pl.ds(device * per, per)]

    def a2a(a, d):
        target = (col + d) % ncol
        return pltpu.make_async_remote_copy(
            src_ref=keys_of(a, target), dst_ref=grad_all.at[a, col],
            send_sem=a2a_send.at[a, d], recv_sem=a2a_recv.at[a, d],
            device_id=(row, target), device_id_type=MESH,
        )

    def a2a_back(a, d):
        source = (col - d) % ncol
        return pltpu.make_async_remote_copy(
            src_ref=keys_of(a, source), dst_ref=grad_all.at[a, source],
            send_sem=a2a_send.at[a, d], recv_sem=a2a_recv.at[a, d],
            device_id=(row, source), device_id_type=MESH,
        )

    keep = []

    def finish_bias(a):
        grad_local[a, 0].wait()
        for n, step in enumerate((1, -1)):
            links.arrived(grad_second[a, step], grad_two.at[a, n])
        add_into(grad_held.at[a, 0], grad_two.at[a, 0], grad_two.at[a, 1])

        def start(d, _):
            a2a(a, d).start()
            return 0

        lax.fori_loop(1, ncol, start, 0)
        keep.append(pltpu.make_async_copy(keys_of(a, col), grad_all.at[a, col], local_sem.at[38 + a]))
        keep[-1].start()

    finish_bias(0)

    tail_one, tail_two = {}, {}
    for i in (2, 1, 3, 0):
        for hf in range(2):
            block = mine[hf, i]
            for n, step in enumerate((1, -1)):
                links.arrived(two[hf, i, step], two_in.at[hf, i, n])
            add_into(block, two_in.at[hf, i, 0], two_in.at[hf, i, 1])
            if i == 2:
                for n, step in enumerate((1, -1)):
                    tail_one[hf, step] = links.send(
                        block.at[sub_of(step)], last_one.at[hf, n], place.along(hf, step)
                    )
            elif i != 0:
                n, step = (0, 1) if i == 1 else (1, -1)
                links.arrived(tail_one[hf, step], last_one.at[hf, n])
                add_into(block.at[sub_of(step)], last_one.at[hf, n])
                tail_two[hf, step] = links.send(block, last_two.at[hf, n], place.along(hf, step))
    finish_bias(1)

    for hf in range(2):
        block = mine[hf, 0]
        for n, step in enumerate((1, -1)):
            links.arrived(tail_two[hf, step], last_two.at[hf, n])
        add_into(block, last_two.at[hf, 0], last_two.at[hf, 1])
        pair_sum[hf] = block[...]

    def a2a_end(d, _):
        for a in range(2):
            a2a_back(a, d).wait_recv()
            a2a(a, d).wait_send()
        return 0

    lax.fori_loop(1, ncol, a2a_end, 0)
    links.arrived(moves[0], out_odd)
    links.arrived(moves[1], dn_odd)
    links.finish()
    for copy in keep:
        copy.wait()


def reduce(pair, bias_grad, out, dn):
    ncol = 8 * RING
    rows, cols, chans = out.shape[1:]
    pair = pair.reshape(ncol, 2, rows, cols, chans)
    keys = bias_grad.shape[1] * TILE // RING
    unit = 32
    grads = bias_grad.reshape(2, RING, keys // unit, unit, HJ)
    part = keys // ncol
    anywhere = pl.BlockSpec(memory_space=pl.ANY)
    vmem = pl.BlockSpec(memory_space=pltpu.VMEM)
    block = (rows, cols, chans)
    half = (rows // 2, cols, chans)
    return pl.pallas_call(
        reduce_kernel,
        out_shape=(
            jax.ShapeDtypeStruct((2,) + block, BF16),
            jax.ShapeDtypeStruct((2, ncol, part // unit, unit, HJ), BF16),
            jax.ShapeDtypeStruct(block, BF16),
            jax.ShapeDtypeStruct(block, BF16),
        ),
        in_specs=[anywhere] * 4,
        out_specs=(vmem, anywhere, anywhere, anywhere),
        scratch_shapes=[
            pltpu.VMEM((RING * RING, 2) + block, BF16),
            pltpu.VMEM((RING * RING, 2) + block, BF16),
            pltpu.VMEM((2, RING, 2) + half, BF16),
            pltpu.VMEM((2, RING, 2) + block, BF16),
            pltpu.VMEM((2, 2) + half, BF16),
            pltpu.VMEM((2, 2) + block, BF16),
            pltpu.VMEM((2, RING, keys // unit, unit, HJ), BF16),
            pltpu.VMEM((2, 2, keys // unit // 2, unit, HJ), BF16),
            pltpu.VMEM((2, 2, keys // unit, unit, HJ), BF16),
            pltpu.SemaphoreType.DMA((40,)),
            pltpu.SemaphoreType.DMA((90,)),
            pltpu.SemaphoreType.DMA((90,)),
            pltpu.SemaphoreType.DMA((2, ncol)),
            pltpu.SemaphoreType.DMA((2, ncol)),
        ],
        compiler_params=pltpu.CompilerParams(
            collective_id=1, has_side_effects=True, vmem_limit_bytes=62 * 1024 * 1024
        ),
        name="reduce",
    )(pair, grads, out, dn)


def finish_kernel(
    slab_ref, out_ref, out_odd_ref, dn_ref, dn_odd_ref, pair_ref, grad_ref,
    attn_ref, slab_grad_ref, bias_grad_ref,
):
    count = grad_ref.shape[1]
    rows = slab_ref.shape[0]
    for m in range(count):
        even = grad_ref[0, m].astype(F32)
        odd = grad_ref[1, count - 1 - m].astype(F32)
        for h in range(H):
            part = slice(h * TILE, (h + 1) * TILE)
            both = jnp.concatenate([even[:, part], odd[:, part]], axis=1)
            bias_grad_ref[:, h, 2 * TILE * m : 2 * TILE * (m + 1)] = both
    for r in range(rows):
        for a in range(2):
            part = slice(a * TILE, (a + 1) * TILE)
            attn_ref[r, part] = out_ref[0, r] if a == 0 else out_odd_ref[r]
            d_own = dn_ref[0, r] if a == 0 else dn_odd_ref[r]
            d_normed = d_own.astype(F32) + pair_ref[a, r].astype(F32)
            normed, scale = normalize(slab_ref[r, part].astype(F32))
            d_mean = jnp.mean(d_normed, axis=-1, keepdims=True)
            d_along = jnp.mean(d_normed * normed, axis=-1, keepdims=True)
            slab_grad_ref[r, part] = (scale * (d_normed - d_mean - normed * d_along)).astype(BF16)


def finish(pair_slab, out, out_odd, dn, dn_odd, pair_sum, grads):
    count, keys = grads.shape[1:3]
    rows, cols, chans = pair_slab.shape
    parts = 2
    whole = pl.BlockSpec((rows // parts, cols, chans), lambda i: (i, 0, 0))
    odd = pl.BlockSpec((rows // parts, TILE, chans), lambda i: (i, 0, 0))
    both = pl.BlockSpec((2, rows // parts, TILE, chans), lambda i: (0, i, 0, 0))
    return pl.pallas_call(
        finish_kernel,
        grid=(parts,),
        out_shape=(
            jax.ShapeDtypeStruct(pair_slab.shape, BF16),
            jax.ShapeDtypeStruct(pair_slab.shape, BF16),
            jax.ShapeDtypeStruct((keys, H, 2 * TILE * count), F32),
        ),
        in_specs=[
            whole, both, odd, both, odd, both,
            pl.BlockSpec((2, count, keys // parts, HJ), lambda i: (0, 0, i, 0)),
        ],
        out_specs=(
            whole, whole,
            pl.BlockSpec((keys // parts, H, 2 * TILE * count), lambda i: (i, 0, 0)),
        ),
        compiler_params=pltpu.CompilerParams(vmem_limit_bytes=62 * 1024 * 1024),
        name="finish",
    )(pair_slab, out, out_odd, dn, dn_odd, pair_sum, grads)


def on_device(pair_slab, pair_bias, tile_mask, w_proj, w_out, d_out):
    ncol = lax.axis_size("col")
    c = lax.axis_index("col")
    x_all, bias_all, d_odd = gather(pair_slab, pair_bias, d_out)
    bias_t = bias_all.reshape(2, -1, TILE, HJ)
    out, dn, pair, bias_grad = attention(
        c.reshape(1).astype(jnp.int32), tile_mask, x_all, bias_t, d_out, d_odd, w_proj, w_out
    )
    pair_sum, grads, out_odd, dn_odd = reduce(pair, bias_grad, out, dn)
    return finish(pair_slab, out, out_odd, dn, dn_odd, pair_sum, grads.reshape(2, ncol, -1, HJ))


def solution(mesh):
    in_specs = (P("row", "col", None), P(None, "col", "row"), P(), P(), P(), P("row", "col", None))
    out_specs = (P("row", "col", None), P("row", "col", None), P(("row", "col"), None, None))
    return jax.shard_map(
        on_device, mesh=mesh, in_specs=in_specs, out_specs=out_specs, check_vma=False
    )
```
